256 devices in a mesh: dp: 8 (over y, core), cuts: 32 (over x, z).
Axes of the slice: x: 4, y: 4, z: 8, core: 2. Of those that a mesh axis runs over, the one named last changes fastest.
Arguments:
- activations: bfloat16 [32768, 4096], P(('dp', 'cuts')), parts along dimension 0, may hold values from -6 to 6
- output_gradients: bfloat16 [32768, 14336], P(('dp', 'cuts')), parts along dimension 0, may hold values from -6 to 6
- adapter_down: bfloat16 [4096, 16], replicated, may hold values from -0.09375 to 0.09375
- adapter_up: bfloat16 [16, 14336], replicated, may hold values from -0.046875 to 0.046875
- token_example_number: int32 [32768], P(('dp', 'cuts')), parts along dimension 0, may hold values from 0 to 63, as said below
- cut_first_example: int32 [264], P('dp'), parts along dimension 0, may hold values from 0 to 64, as said below
- block_seeds: int32 [32], replicated, may hold values from 0 to 1073741823
Outputs:
- features: float32 [512, 4096], P(('dp', 'cuts')), parts along dimension 0
The draws below stay inside these ranges and needn't reach their ends.
There are 8 independent parts, one for each index of `dp`. The reference program is written for one: setup_inputs(seed, part) draws one part's arguments, and reference() takes and returns one part's arrays. A program takes and returns all parts, laid end to end along the dimension named above; an argument that names none is the same for every part. Nothing has to cross between parts.
Inputs may be any that keep to these rules, and one draw needn't show every extreme that they name: `token_example_number`: within the 128 rows of each index d of cuts the example numbers never fall and take every value from cut_first_example[d] to cut_first_example[d+1] - 1; no example spans two indices. `cut_first_example`: starts at 0, ends at 64; each index of cuts holds 1 to 4 examples and some index holds exactly 4.
All inputs are finite; a program needn't handle non-finite values.
Results may differ from the reference program's by a relative error of at most 0.0041.
Values may be sent and summed in bfloat16 or wider, within the bound.
No kernel may reach another device: no remote copies, remote signals or barrier semaphores. Data moves between devices by JAX's collectives and lax.ppermute only.
A program may use at most 128 MiB of HBM per device.

```python
import jax
import jax.numpy as jnp
from jax import lax

MODEL_WIDTH = 4096
HIDDEN_UNITS = 14336
ADAPTER_RANK = 16
SKETCH = 4096
BLOCKS = 32
PANEL = 256
TOK_DEV = 128
EXMAX = 4
EX_AVG = 2
TOKENS = 4096
EXAMPLES = 64
N_CUTS = 32


def example_layout(key):
    pick_key, order_key, cut_key = jax.random.split(key, 3)
    heavy = jax.random.randint(pick_key, (), 0, N_CUTS)
    others = N_CUTS - 1
    extra = EX_AVG * N_CUTS - EXMAX - others
    ranking = jax.random.permutation(order_key, N_CUTS).astype(jnp.int32)
    ranking = jnp.where(ranking > ranking[heavy], ranking - 1, ranking)
    counts = 1 + extra // others + (ranking < extra % others).astype(jnp.int32)
    counts = jnp.where(lax.iota(jnp.int32, N_CUTS) == heavy, EXMAX, counts).astype(jnp.int32)
    cut_first_example = jnp.concatenate([jnp.zeros((1,), jnp.int32), jnp.cumsum(counts).astype(jnp.int32)])
    scores = jax.random.randint(cut_key, (N_CUTS, TOK_DEV - 1), 0, 1 << 20) * TOK_DEV + lax.iota(jnp.int32, TOK_DEV - 1)[None, :]
    order = jnp.argsort(-scores, axis=1, stable=True)
    ranks = jnp.argsort(order, axis=1, stable=True).astype(jnp.int32)
    boundary = (ranks < counts[:, None] - 1).astype(jnp.int32)
    local_ids = jnp.concatenate([jnp.zeros((N_CUTS, 1), jnp.int32), jnp.cumsum(boundary, axis=1).astype(jnp.int32)], axis=1)
    token_example_number = (cut_first_example[:N_CUTS, None] + local_ids).reshape(N_CUTS * TOK_DEV)
    return (token_example_number.astype(jnp.int32), cut_first_example)


def draw_token_example_number(key, part):
    return example_layout(key)[0]


def draw_cut_first_example(key, part):
    return example_layout(key)[1]


def set_ends(result, stream_key, smallest, high):
    shape = result.shape
    place = [jax.random.randint(jax.random.fold_in(stream_key, axis), (), 0, shape[axis]) for axis in range(len(shape))]
    result = result.at[tuple(place)].set(smallest)
    longest = shape.index(max(shape))
    place[longest] = (place[longest] + 1) % shape[longest]
    return result.at[tuple(place)].set(high)


def block_scale(rng, extent, cuts, least, largest):
    gain = 1.0
    for axis_at, shards_of in cuts:
        heights = jax.random.uniform(jax.random.fold_in(jax.random.fold_in(rng, 6), axis_at), (shards_of,), jnp.float32, least / len(cuts), largest / len(cuts))
        gain = gain * jnp.repeat(jnp.exp(heights), extent[axis_at] // shards_of).reshape((-1,) + (1,) * (len(extent) - 1 - axis_at))
    return gain


def normal_values(own_key, dims, scale, bound, shards=(), kind=jnp.bfloat16):
    gain = block_scale(own_key, dims, shards, -0.22, 0.18) if shards else 1.0
    values = jax.random.normal(own_key, dims, jnp.float32) * scale * gain
    return jnp.minimum(jnp.maximum(values, -bound), bound).astype(kind)


def setup_inputs(seed: int = 0, part: int = 0) -> dict:
    keys = jax.random.split(jax.random.key(seed), 8)
    part_splits = jax.random.split(jax.random.fold_in(keys[7], part), 8)
    activations = normal_values(part_splits[0], (TOKENS, MODEL_WIDTH), 1.0, 6.0, ((0, 32),))
    output_gradients = normal_values(part_splits[1], (TOKENS, HIDDEN_UNITS), 1.0, 6.0, ((0, 32),))
    adapter_down = normal_values(keys[2], (MODEL_WIDTH, ADAPTER_RANK), MODEL_WIDTH ** -0.5, 0.09375)
    adapter_up = normal_values(keys[3], (ADAPTER_RANK, HIDDEN_UNITS), HIDDEN_UNITS ** -0.5, 0.046875)
    token_example_number = draw_token_example_number(jax.random.fold_in(jax.random.fold_in(keys[7], part), 71), part)
    cut_first_example = draw_cut_first_example(jax.random.fold_in(jax.random.fold_in(keys[7], part), 71), part)
    block_seeds = set_ends(jax.random.randint(keys[6], (BLOCKS,), 0, 2**30), jax.random.fold_in(keys[6], 1), 0, (2**30) - 1).astype(jnp.int32)
    return dict(activations=activations, output_gradients=output_gradients, adapter_down=adapter_down, adapter_up=adapter_up, token_example_number=token_example_number, cut_first_example=cut_first_example, block_seeds=block_seeds)


def rademacher(seed_value, first_row, row_count, col_count):
    feature_ids = (first_row + lax.iota(jnp.int32, row_count))[:, None]
    param_ids = lax.iota(jnp.int32, col_count)[None, :]
    mixed = param_ids * 1640531527 + feature_ids * 668265263 + seed_value
    mixed = mixed ^ (jnp.right_shift(mixed, 15) & 131071)
    mixed = mixed * 739982445
    mixed = mixed ^ (jnp.right_shift(mixed, 13) & 524287)
    picked = jnp.right_shift(mixed, 20) & 1
    return (2 * picked - 1).astype(jnp.bfloat16)


def example_rows(cut_first_example, owners, slot_cap, example_total):
    example_ids = lax.iota(jnp.int32, example_total)
    holder = jnp.sum((cut_first_example[None, 1:owners + 1] <= example_ids[:, None]).astype(jnp.int32), axis=1)
    start_ids = jnp.take(cut_first_example, holder)
    return (holder * slot_cap + example_ids - start_ids).astype(jnp.int32)


def reference(activations, output_gradients, adapter_down, adapter_up, token_example_number, cut_first_example, block_seeds):
    acts_split = activations.reshape(N_CUTS, TOK_DEV, MODEL_WIDTH)
    grads_split = output_gradients.reshape(N_CUTS, TOK_DEV, HIDDEN_UNITS)
    tokens_split = token_example_number.reshape(N_CUTS, TOK_DEV)

    def one_device(packed):
        local_activations, local_gradients, ids_here, first_here = packed
        up_matrix = jnp.dot(local_gradients, adapter_up.T, preferred_element_type=jnp.float32).astype(jnp.bfloat16)
        down_matrix = jnp.dot(local_activations, adapter_down, preferred_element_type=jnp.float32).astype(jnp.bfloat16)
        slot_ids = ids_here - first_here
        onehot = (slot_ids[:, None] == lax.iota(jnp.int32, EXMAX)[None, :]).astype(jnp.bfloat16)
        spread_up = (up_matrix[:, None, :] * onehot[:, :, None]).reshape(TOK_DEV, EXMAX * ADAPTER_RANK)
        spread_down = (down_matrix[:, None, :] * onehot[:, :, None]).reshape(TOK_DEV, EXMAX * ADAPTER_RANK)
        grad_a = jnp.dot(spread_up.T, local_activations, preferred_element_type=jnp.float32).astype(jnp.bfloat16)
        grad_b = jnp.dot(spread_down.T, local_gradients, preferred_element_type=jnp.float32).astype(jnp.bfloat16)
        return grad_a.reshape(EXMAX, ADAPTER_RANK, MODEL_WIDTH), grad_b.reshape(EXMAX, ADAPTER_RANK, HIDDEN_UNITS)

    slots_a, slots_b = lax.map(one_device, (acts_split, grads_split, tokens_split, cut_first_example[:N_CUTS]))
    picked = example_rows(cut_first_example, N_CUTS, EXMAX, EXAMPLES)
    grad_a = jnp.take(slots_a.reshape(N_CUTS * EXMAX, ADAPTER_RANK, MODEL_WIDTH), picked, axis=0)
    grad_b = jnp.take(slots_b.reshape(N_CUTS * EXMAX, ADAPTER_RANK, HIDDEN_UNITS), picked, axis=0)
    a_width = MODEL_WIDTH // BLOCKS
    b_width = HIDDEN_UNITS // BLOCKS
    block_len = ADAPTER_RANK * (a_width + b_width)

    def one_block(carry, block_idx):
        part_a = lax.dynamic_slice_in_dim(grad_a, block_idx * a_width, a_width, 2).reshape(EXAMPLES, ADAPTER_RANK * a_width)
        part_b = lax.dynamic_slice_in_dim(grad_b, block_idx * b_width, b_width, 2).reshape(EXAMPLES, ADAPTER_RANK * b_width)
        vector = jnp.concatenate([part_a, part_b], axis=1).astype(jnp.float32)
        seed_value = block_seeds[block_idx]

        def one_panel(panel_idx):
            signs = rademacher(seed_value, panel_idx * PANEL, PANEL, block_len).astype(jnp.float32)
            return jnp.dot(vector, signs.T, precision=lax.Precision.HIGHEST)

        pieces = lax.map(one_panel, jnp.arange(SKETCH // PANEL, dtype=jnp.int32))
        return carry + jnp.moveaxis(pieces, 0, 1).reshape(EXAMPLES, SKETCH), None

    total, unused_out = lax.scan(one_block, jnp.zeros((EXAMPLES, SKETCH), jnp.float32), jnp.arange(BLOCKS, dtype=jnp.int32))
    return total * (float(ADAPTER_RANK * (MODEL_WIDTH + HIDDEN_UNITS) * TOK_DEV) ** -0.5)
```

```python
import functools

import jax
import jax.numpy as jnp
import numpy as np
from jax import lax
from jax.experimental import pallas as pl
from jax.experimental.pallas import tpu as pltpu
from jax.sharding import Mesh
from jax.sharding import PartitionSpec as P

MODEL_WIDTH = 4096
HIDDEN_UNITS = 14336
RANK = 16
SKETCH = 4096
BLOCKS = 32
TOK_DEV = 128
EXMAX = 4
EXAMPLES = 64
NY, NCORE, NX, NZ = 4, 2, 4, 8
CHIPS = NY * NX
COLS = (MODEL_WIDTH + HIDDEN_UNITS) // CHIPS
ROWS = EXMAX * RANK
LANES = 128
TILES = COLS // LANES
A_WIDTH = MODEL_WIDTH // BLOCKS
B_WIDTH = HIDDEN_UNITS // BLOCKS
PAIRS = RANK // 2
SLOTS = NCORE * CHIPS * EXMAX
KDEV = SKETCH // NCORE
KTILE = KDEV // NX
CUT_SLOTS = NX * EXMAX
PIECES = NCORE * KTILE // LANES


def as_i32(value):
    value &= 0xFFFFFFFF
    return np.int32(value - (1 << 32) if value >= 1 << 31 else value)


Q_STEP = 1640531527
K_STEP = 668265263
MULT = as_i32(739982445 << 11)
NT = (((1,), (1,)), ((), ()))
F32 = jnp.float32
BF16 = jnp.bfloat16
I32 = jnp.int32


def iota(shape, dim):
    return lax.broadcasted_iota(I32, shape, dim)


def gradient_kernel(tok_ref, first_ref, cut_ref, act_ref, gout_ref, down_ref, up_ref, out_ref):
    up = lax.dot_general(gout_ref[...], up_ref[...], NT, preferred_element_type=F32).astype(BF16)
    down = jnp.dot(act_ref[...], down_ref[...], preferred_element_type=F32).astype(BF16)
    slot = tok_ref[...] - first_ref[cut_ref[0]]
    expand = (lax.rem(iota((ROWS, RANK), 0), RANK) == iota((ROWS, RANK), 1)).astype(F32).astype(BF16)
    mine = (iota((ROWS, TOK_DEV), 0) // RANK) == slot

    def spread(factor):
        rows = lax.dot_general(expand, factor, NT, preferred_element_type=F32)
        return jnp.where(mine, rows, 0.0).astype(BF16)

    spread_up, spread_down = spread(up), spread(down)
    for chip in range(CHIPS):
        lo, hi = chip * COLS, (chip + 1) * COLS
        mid = min(max(MODEL_WIDTH, lo), hi)
        if mid > lo:
            part = jnp.dot(spread_up, act_ref[:, lo:mid], preferred_element_type=F32)
            out_ref[chip, :, : mid - lo] = part.astype(BF16)
        if hi > mid:
            part = jnp.dot(
                spread_down,
                gout_ref[:, mid - MODEL_WIDTH : hi - MODEL_WIDTH],
                preferred_element_type=F32,
            )
            out_ref[chip, :, mid - lo :] = part.astype(BF16)


def sketch_kernel(where_ref, seeds_ref, own_ref, partner_ref, out_ref, vec_ref, base_ref, acc_ref):
    step = pl.program_id(0)
    chip, core = where_ref[0], where_ref[1]

    @pl.when(step == 0)
    def _():
        to, at = iota((256, 256), 0), iota((256, 256), 1)
        source = lax.rem(to, 16) // EXMAX * ROWS + lax.rem(to, EXMAX) * RANK + to // 16
        order = (at == source).astype(F32).astype(BF16)
        for half, ref in enumerate((own_ref, partner_ref)):
            for y in range(NY):
                rows = ref[NX * y : NX * (y + 1)].reshape(NX * ROWS, COLS)
                rows = jnp.dot(order, rows, preferred_element_type=F32).astype(BF16)
                lo = half * CHIPS * EXMAX + y * CUT_SLOTS
                for r in range(RANK):
                    vec_ref[r // 2, lo : lo + CUT_SLOTS, (r % 2) * COLS : (r % 2 + 1) * COLS] = rows[
                        r * CUT_SLOTS : (r + 1) * CUT_SLOTS
                    ]
        lane = iota((8, LANES), 1)
        for tile in range(TILES):
            column = chip * COLS + tile * LANES
            is_a = column < MODEL_WIDTH
            f = jnp.maximum(column - MODEL_WIDTH, 0)
            width = jnp.where(is_a, A_WIDTH, B_WIDTH)
            block = jnp.where(is_a, column // A_WIDTH, f // B_WIDTH)
            into = jnp.where(is_a, 0, f - f // B_WIDTH * B_WIDTH)
            after = jnp.minimum(block + 1, BLOCKS - 1)
            place = lane + into
            over = place >= width
            seed = jnp.where(over, seeds_ref[after], seeds_ref[block])
            place = jnp.where(over, place - width, place)
            start = jnp.where(is_a, 0, RANK * A_WIDTH)
            base = (place + start) * as_i32(Q_STEP) + seed
            for r in range(RANK):
                lo = (r % 2) * COLS + tile * LANES
                base_ref[r // 2, :, lo : lo + LANES] = base + (width * r) * as_i32(Q_STEP)

    feature = (iota((16, LANES), 0) + (core * KDEV + step * KTILE)) * as_i32(K_STEP)
    acc_ref[...] = jnp.zeros_like(acc_ref)

    def pair(p, carry):
        base = []
        for tile in range(2 * TILES):
            eight = base_ref[p, :, tile * LANES : (tile + 1) * LANES]
            base.append(jnp.concatenate([eight, eight], axis=0))
        rows = []
        for k in range(0, KTILE, 16):
            here = feature + as_i32(k * K_STEP)
            signs = []
            for tile in range(2 * TILES):
                h = base[tile] + here
                h = (h ^ lax.shift_right_logical(h, np.int32(15))) * MULT
                signs.append(jnp.where(h < 0, BF16(1), BF16(-1)))
            rows.append(jnp.concatenate(signs, axis=1))
        acc_ref[...] += lax.dot_general(
            jnp.concatenate(rows, axis=0), vec_ref[p], NT, preferred_element_type=F32
        )
        return carry

    lax.fori_loop(0, PAIRS, pair, 0)
    total = acc_ref[...].T.astype(BF16)
    for half in range(NCORE):
        to_core = core if half == 0 else 1 - core
        for y in range(NY):
            lo = half * CHIPS * EXMAX + y * CUT_SLOTS
            out_ref[y, to_core, 0] = total[lo : lo + CUT_SLOTS]


def route_kernel(first_ref, z_ref, in_ref, out_ref):
    sums = []
    for c in range(NCORE):
        total = jnp.zeros((CUT_SLOTS, KTILE), F32)
        for y in range(NY):
            for x in range(NX):
                total = total + in_ref[(y * NCORE + c) * NX + x].astype(F32)
        sums.append(total.astype(BF16))
    stacked = jnp.concatenate(
        [
            sums[c][:, u * LANES : (u + 1) * LANES]
            for c in range(NCORE)
            for u in range(KTILE // LANES)
        ],
        axis=0,
    )
    z = z_ref[0]
    width = PIECES * CUT_SLOTS
    row, col = iota((EXAMPLES * PIECES, width), 0), iota((EXAMPLES * PIECES, width), 1)
    slot = lax.rem(col, CUT_SLOTS)
    example = jnp.full(row.shape, -1, I32)
    for x in range(NX):
        cut = x * NZ + z
        number = first_ref[cut] + lax.rem(slot, EXMAX)
        number = jnp.where(number < first_ref[cut + 1], number, -1)
        example = jnp.where(slot // EXMAX == x, number, example)
    hit = (row // PIECES == example) & (lax.rem(row, PIECES) == col // CUT_SLOTS)
    routed = jnp.dot(hit.astype(F32).astype(BF16), stacked, preferred_element_type=F32)
    out_ref[...] = routed.astype(BF16).reshape(out_ref.shape)


def finish_kernel(in_ref, out_ref):
    scale = float(RANK * (MODEL_WIDTH + HIDDEN_UNITS) * TOK_DEV) ** (-0.5)
    per = KTILE // LANES
    for x in range(NX):
        total = jnp.zeros(in_ref.shape[1:], F32)
        for z in range(NZ):
            total = total + in_ref[x * NZ + z].astype(F32)
        total = total * scale
        for p in range(2):
            for c in range(NCORE):
                for u in range(per):
                    row = p * PIECES + c * per + u
                    lo = c * KDEV + x * KTILE + u * LANES
                    out_ref[p : p + 1, lo : lo + LANES] = total[row : row + 1]


VMEM = pl.BlockSpec(memory_space=pltpu.VMEM)
SMEM = pl.BlockSpec(memory_space=pltpu.SMEM)


def params(mib):
    return pltpu.CompilerParams(vmem_limit_bytes=mib << 20)


def body(acts, gouts, adapter_down, adapter_up, token_example, cut_first, seeds):
    y, core, x, z = (lax.axis_index(name) for name in ("y", "core", "x", "z"))
    cut = (x * NZ + z).astype(I32).reshape(1)
    grads = pl.pallas_call(
        gradient_kernel,
        out_shape=jax.ShapeDtypeStruct((CHIPS, ROWS, COLS), BF16),
        in_specs=[VMEM, SMEM, SMEM, VMEM, VMEM, VMEM, VMEM],
        out_specs=VMEM,
        compiler_params=params(40),
        name="gradients",
    )(token_example.reshape(1, TOK_DEV), cut_first, cut, acts, gouts, adapter_down, adapter_up)
    own = lax.all_to_all(grads, ("y", "x"), 0, 0, tiled=True)
    partner = lax.ppermute(own, "core", [(0, 1), (1, 0)])
    where = jnp.stack([(y * NX + x).astype(I32), core.astype(I32)])
    whole = lambda i: (0, 0, 0)
    parts = pl.pallas_call(
        sketch_kernel,
        grid=(NX,),
        out_shape=jax.ShapeDtypeStruct((NY, NCORE, NX, CUT_SLOTS, KTILE), BF16),
        in_specs=[
            SMEM,
            SMEM,
            pl.BlockSpec((CHIPS, ROWS, COLS), whole),
            pl.BlockSpec((CHIPS, ROWS, COLS), whole),
        ],
        out_specs=pl.BlockSpec((NY, NCORE, 1, CUT_SLOTS, KTILE), lambda i: (0, 0, i, 0, 0)),
        scratch_shapes=[
            pltpu.VMEM((PAIRS, SLOTS, 2 * COLS), BF16),
            pltpu.VMEM((PAIRS, 8, 2 * COLS), I32),
            pltpu.VMEM((KTILE, SLOTS), F32),
        ],
        compiler_params=params(48),
        name="sketch",
    )(where, seeds, own, partner)
    parts = parts.reshape(NY * NCORE * NX, CUT_SLOTS, KTILE)
    parts = lax.all_to_all(parts, ("y", "core", "x"), 0, 0, tiled=True)
    routed = pl.pallas_call(
        route_kernel,
        out_shape=jax.ShapeDtypeStruct((NX * NZ, 2 * PIECES, LANES), BF16),
        in_specs=[SMEM, SMEM, VMEM],
        out_specs=VMEM,
        compiler_params=params(32),
        name="route",
    )(cut_first, z.astype(I32).reshape(1), parts)
    routed = lax.all_to_all(routed, ("x", "z"), 0, 0, tiled=True)
    return pl.pallas_call(
        finish_kernel,
        out_shape=jax.ShapeDtypeStruct((2, SKETCH), F32),
        in_specs=[VMEM],
        out_specs=VMEM,
        compiler_params=params(32),
        name="finish",
    )(routed)


def solution(mesh):
    fine = Mesh(mesh.devices.reshape(NY, NCORE, NX, NZ), ("y", "core", "x", "z"))
    every = ("y", "core", "x", "z")
    in_specs = (P(every, None), P(every, None), P(), P(), P(every), P(("y", "core")), P())
    return jax.shard_map(body, mesh=fine, in_specs=in_specs, out_specs=P(every, None), check_vma=False)
```

```python
import jax
import jax.numpy as jnp
import numpy as np
from jax import lax
from jax.experimental import pallas as pl
from jax.experimental.pallas import tpu as pltpu
from jax.sharding import Mesh
from jax.sharding import PartitionSpec as P

MODEL_WIDTH = 4096
HIDDEN_UNITS = 14336
RANK = 16
SKETCH = 4096
BLOCKS = 32
TOK_DEV = 128
EXMAX = 4
EXAMPLES = 64
NY, NCORE, NX, NZ = 4, 2, 4, 8
CHIPS = NY * NX
COLS = (MODEL_WIDTH + HIDDEN_UNITS) // CHIPS
ROWS = EXMAX * RANK
LANES = 128
TILES = COLS // LANES
A_WIDTH = MODEL_WIDTH // BLOCKS
B_WIDTH = HIDDEN_UNITS // BLOCKS
PAIRS = RANK // 2
SLOTS = NCORE * CHIPS * EXMAX
KDEV = SKETCH // NCORE
KTILE = KDEV // NX
CUT_SLOTS = NX * EXMAX
PIECES = NCORE * KTILE // LANES
GROUPS = (3, 6, 9, 13, 16)
EARLY = PAIRS // 2


def as_i32(value):
    value &= 0xFFFFFFFF
    return np.int32(value - (1 << 32) if value >= 1 << 31 else value)


Q_STEP = 1640531527
K_STEP = 668265263
MULT = as_i32(739982445 << 11)
NT = (((1,), (1,)), ((), ()))
F32 = jnp.float32
BF16 = jnp.bfloat16
I32 = jnp.int32


def iota(shape, dim):
    return lax.broadcasted_iota(I32, shape, dim)


def gradient_kernel(
    tok_hbm, first_hbm, act_hbm, gout_hbm, down_hbm, up_hbm, out_ref,
    tok_ref, first_ref, act_ref, gout_ref, down_ref, up_ref, sems,
):
    copies = [
        pltpu.make_async_copy(src, dst, sems.at[i])
        for i, (src, dst) in enumerate(
            (
                (down_hbm, down_ref),
                (act_hbm, act_ref),
                (tok_hbm, tok_ref),
                (first_hbm, first_ref),
                (up_hbm, up_ref),
            )
        )
    ]
    for lo, hi in zip(GROUPS[:-1], GROUPS[1:]):
        columns = slice(max(lo * COLS - MODEL_WIDTH, 0), hi * COLS - MODEL_WIDTH)
        copies.append(
            pltpu.make_async_copy(
                gout_hbm.at[:, columns], gout_ref.at[:, columns], sems.at[len(copies)]
            )
        )
    for copy in copies:
        copy.start()
    expand = (lax.rem(iota((ROWS, RANK), 0), RANK) == iota((ROWS, RANK), 1)).astype(F32).astype(BF16)
    for copy in copies[:4]:
        copy.wait()
    cut = lax.axis_index("x") * NZ + lax.axis_index("z")
    slot = tok_ref[...] - first_ref[cut]
    mine = (iota((ROWS, TOK_DEV), 0) // RANK) == slot

    def spread(factor):
        rows = lax.dot_general(expand, factor.astype(BF16), NT, preferred_element_type=F32)
        return jnp.where(mine, rows, 0.0).astype(BF16)

    spread_down = spread(
        lax.dot_general(act_ref[...], down_ref[...], NT, preferred_element_type=F32)
    )
    copies[4].wait()
    up = jnp.zeros((TOK_DEV, RANK), F32)
    for group, (first, last) in enumerate(zip(GROUPS[:-1], GROUPS[1:])):
        copies[5 + group].wait()
        for chip in range(first, last):
            lo, hi = max(chip * COLS - MODEL_WIDTH, 0), (chip + 1) * COLS - MODEL_WIDTH
            up = up + lax.dot_general(
                gout_ref[:, lo:hi], up_ref[:, lo:hi], NT, preferred_element_type=F32
            )
            part = jnp.dot(spread_down, gout_ref[:, lo:hi], preferred_element_type=F32)
            out_ref[chip, :, COLS - (hi - lo) :] = part.astype(BF16)
    spread_up = spread(up)
    for chip in range(GROUPS[0] + 1):
        lo, hi = chip * COLS, min((chip + 1) * COLS, MODEL_WIDTH)
        part = jnp.dot(spread_up, act_ref[:, lo:hi], preferred_element_type=F32)
        out_ref[chip, :, : hi - lo] = part.astype(BF16)


def signs_of(base_ref, p, feature):
    base = []
    for tile in range(2 * TILES):
        eight = base_ref[p, :, tile * LANES : (tile + 1) * LANES]
        base.append(jnp.concatenate([eight, eight], axis=0))
    for k in range(0, KTILE, 16):
        here = feature + as_i32(k * K_STEP)
        signs = []
        for tile in range(2 * TILES):
            h = base[tile] + here
            h = (h ^ lax.shift_right_logical(h, np.int32(15))) * MULT
            signs.append(jnp.where(h < 0, BF16(1), BF16(-1)))
        yield k, jnp.concatenate(signs, axis=1)


def first_feature(core, step):
    return (iota((16, LANES), 0) + (core * KDEV + step * KTILE)) * as_i32(K_STEP)


def sign_kernel(where_ref, seeds_ref, base_ref, sign_hbm, made_ref, sems):
    chip, core = where_ref[0], where_ref[1]
    lane = iota((8, LANES), 1)
    for tile in range(TILES):
        column = chip * COLS + tile * LANES
        is_a = column < MODEL_WIDTH
        f = jnp.maximum(column - MODEL_WIDTH, 0)
        width = jnp.where(is_a, A_WIDTH, B_WIDTH)
        block = jnp.where(is_a, column // A_WIDTH, f // B_WIDTH)
        into = jnp.where(is_a, 0, f - f // B_WIDTH * B_WIDTH)
        after = jnp.minimum(block + 1, BLOCKS - 1)
        place = lane + into
        over = place >= width
        seed = jnp.where(over, seeds_ref[after], seeds_ref[block])
        place = jnp.where(over, place - width, place)
        start = jnp.where(is_a, 0, RANK * A_WIDTH)
        base = (place + start) * as_i32(Q_STEP) + seed
        for r in range(RANK):
            lo = (r % 2) * COLS + tile * LANES
            base_ref[r // 2, :, lo : lo + LANES] = base + (width * r) * as_i32(Q_STEP)

    def send(i):
        slot = lax.rem(i, 2)
        return pltpu.make_async_copy(made_ref.at[slot], sign_hbm.at[i], sems.at[slot])

    def fill(i, carry):
        @pl.when(i >= 2)
        def _():
            send(i - 2).wait()

        slot = lax.rem(i, 2)
        tile, p = i // EARLY, lax.rem(i, EARLY)
        for k, signs in signs_of(base_ref, p, first_feature(core, tile)):
            made_ref[slot, k : k + 16] = signs
        send(i).start()
        return carry

    lax.fori_loop(0, NX * EARLY, fill, 0)
    send(NX * EARLY - 2).wait()
    send(NX * EARLY - 1).wait()


def sketch_kernel(
    where_ref, base_ref, sign_hbm, own_ref, partner_ref, out_ref, vec_ref, acc_ref, sign_ref, sems
):
    core = where_ref[1]

    def fetch(i):
        slot = lax.rem(i, 3)
        return pltpu.make_async_copy(sign_hbm.at[i], sign_ref.at[slot], sems.at[slot])

    fetch(0).start()
    fetch(1).start()
    to, at = iota((256, 256), 0), iota((256, 256), 1)
    source = lax.rem(to, 16) // EXMAX * ROWS + lax.rem(to, EXMAX) * RANK + to // 16
    order = (at == source).astype(F32).astype(BF16)
    for half, ref in enumerate((own_ref, partner_ref)):
        for y in range(NY):
            rows = ref[NX * y : NX * (y + 1)].reshape(NX * ROWS, COLS)
            rows = jnp.dot(order, rows, preferred_element_type=F32).astype(BF16)
            lo = half * CHIPS * EXMAX + y * CUT_SLOTS
            for r in range(RANK):
                vec_ref[r // 2, lo : lo + CUT_SLOTS, (r % 2) * COLS : (r % 2 + 1) * COLS] = rows[
                    r * CUT_SLOTS : (r + 1) * CUT_SLOTS
                ]

    def tile(step, carry):
        feature = first_feature(core, step)
        acc_ref[...] = jnp.zeros_like(acc_ref)

        def pair(i, carry):
            n = step * EARLY + i

            @pl.when(n + 2 < NX * EARLY)
            def _():
                fetch(n + 2).start()

            fetch(n).wait()
            early = lax.dot_general(
                sign_ref[lax.rem(n, 3)], vec_ref[i], NT, preferred_element_type=F32
            )
            late = jnp.concatenate([rows for _, rows in signs_of(base_ref, EARLY + i, feature)], axis=0)
            late = lax.dot_general(late, vec_ref[EARLY + i], NT, preferred_element_type=F32)
            acc_ref[...] += early + late
            return carry

        lax.fori_loop(0, EARLY, pair, 0)
        total = acc_ref[...].T.astype(BF16)
        for half in range(NCORE):
            to_core = core if half == 0 else 1 - core
            for y in range(NY):
                lo = half * CHIPS * EXMAX + y * CUT_SLOTS
                out_ref[y, to_core, step] = total[lo : lo + CUT_SLOTS]
        return carry

    lax.fori_loop(0, NX, tile, 0)


def route_kernel(first_ref, z_ref, in_ref, out_ref):
    sums = []
    for c in range(NCORE):
        total = jnp.zeros((CUT_SLOTS, KTILE), F32)
        for y in range(NY):
            for x in range(NX):
                total = total + in_ref[(y * NCORE + c) * NX + x].astype(F32)
        sums.append(total.astype(BF16))
    stacked = jnp.concatenate(
        [
            sums[c][:, u * LANES : (u + 1) * LANES]
            for c in range(NCORE)
            for u in range(KTILE // LANES)
        ],
        axis=0,
    )
    z = z_ref[0]
    width = PIECES * CUT_SLOTS
    row, col = iota((EXAMPLES * PIECES, width), 0), iota((EXAMPLES * PIECES, width), 1)
    slot = lax.rem(col, CUT_SLOTS)
    example = jnp.full(row.shape, -1, I32)
    for x in range(NX):
        cut = x * NZ + z
        number = first_ref[cut] + lax.rem(slot, EXMAX)
        number = jnp.where(number < first_ref[cut + 1], number, -1)
        example = jnp.where(slot // EXMAX == x, number, example)
    hit = (row // PIECES == example) & (lax.rem(row, PIECES) == col // CUT_SLOTS)
    routed = jnp.dot(hit.astype(F32).astype(BF16), stacked, preferred_element_type=F32)
    out_ref[...] = routed.astype(BF16).reshape(out_ref.shape)


def finish_kernel(in_ref, out_ref):
    scale = float(RANK * (MODEL_WIDTH + HIDDEN_UNITS) * TOK_DEV) ** (-0.5)
    per = KTILE // LANES
    for x in range(NX):
        total = jnp.zeros(in_ref.shape[1:], F32)
        for z in range(NZ):
            total = total + in_ref[x * NZ + z].astype(F32)
        total = total * scale
        for p in range(2):
            for c in range(NCORE):
                for u in range(per):
                    row = p * PIECES + c * per + u
                    lo = c * KDEV + x * KTILE + u * LANES
                    out_ref[p : p + 1, lo : lo + LANES] = total[row : row + 1]


VMEM = pl.BlockSpec(memory_space=pltpu.VMEM)
SMEM = pl.BlockSpec(memory_space=pltpu.SMEM)
HBM = pl.BlockSpec(memory_space=pltpu.HBM)


def in_hbm(array):
    return pltpu.with_memory_space_constraint(array, pltpu.HBM)


def params(mib):
    return pltpu.CompilerParams(vmem_limit_bytes=mib << 20)


def body(acts, gouts, adapter_down, adapter_up, token_example, cut_first, seeds):
    y, core, x, z = (lax.axis_index(name) for name in ("y", "core", "x", "z"))
    grads = pl.pallas_call(
        gradient_kernel,
        out_shape=pltpu.HBM((CHIPS, ROWS, COLS), BF16),
        in_specs=[HBM] * 6,
        out_specs=VMEM,
        scratch_shapes=[
            pltpu.VMEM((1, TOK_DEV), I32),
            pltpu.SMEM((cut_first.shape[0],), I32),
            pltpu.VMEM(acts.shape, BF16),
            pltpu.VMEM(gouts.shape, BF16),
            pltpu.VMEM((RANK, MODEL_WIDTH), BF16),
            pltpu.VMEM(adapter_up.shape, BF16),
            pltpu.SemaphoreType.DMA((5 + len(GROUPS) - 1,)),
        ],
        compiler_params=params(16),
        name="gradients",
    )(*(in_hbm(a) for a in (token_example.reshape(1, TOK_DEV), cut_first, acts, gouts, adapter_down.T, adapter_up)))
    where = jnp.stack([(y * NX + x).astype(I32), core.astype(I32)])
    where, seeds, grads = lax.optimization_barrier((where, seeds, grads))
    own = lax.all_to_all(grads, ("y", "x"), 0, 0, tiled=True)
    base, early = pl.pallas_call(
        sign_kernel,
        out_shape=(
            pltpu.VMEM((PAIRS, 8, 2 * COLS), I32),
            pltpu.HBM((NX * EARLY, KTILE, 2 * COLS), BF16),
        ),
        in_specs=[SMEM, SMEM],
        out_specs=(VMEM, HBM),
        scratch_shapes=[
            pltpu.VMEM((2, KTILE, 2 * COLS), BF16),
            pltpu.SemaphoreType.DMA((2,)),
        ],
        cost_estimate=pl.CostEstimate(flops=20_000_000_000, bytes_accessed=0, transcendentals=0),
        compiler_params=params(16),
        name="signs",
    )(where, seeds)
    own, base = lax.optimization_barrier((own, base))
    partner = lax.ppermute(own, "core", [(0, 1), (1, 0)])
    parts = pl.pallas_call(
        sketch_kernel,
        out_shape=jax.ShapeDtypeStruct((NY, NCORE, NX, CUT_SLOTS, KTILE), BF16),
        in_specs=[SMEM, VMEM, HBM, VMEM, VMEM],
        out_specs=VMEM,
        scratch_shapes=[
            pltpu.VMEM((PAIRS, SLOTS, 2 * COLS), BF16),
            pltpu.VMEM((KTILE, SLOTS), F32),
            pltpu.VMEM((3, KTILE, 2 * COLS), BF16),
            pltpu.SemaphoreType.DMA((3,)),
        ],
        compiler_params=params(32),
        name="sketch",
    )(where, base, in_hbm(early), own, partner)
    parts = parts.reshape(NY * NCORE * NX, CUT_SLOTS, KTILE)
    parts = lax.all_to_all(parts, ("y", "core", "x"), 0, 0, tiled=True)
    routed = pl.pallas_call(
        route_kernel,
        out_shape=jax.ShapeDtypeStruct((NX * NZ, 2 * PIECES, LANES), BF16),
        in_specs=[SMEM, SMEM, VMEM],
        out_specs=VMEM,
        compiler_params=params(32),
        name="route",
    )(cut_first, z.astype(I32).reshape(1), parts)
    routed = lax.all_to_all(routed, ("x", "z"), 0, 0, tiled=True)
    return pl.pallas_call(
        finish_kernel,
        out_shape=jax.ShapeDtypeStruct((2, SKETCH), F32),
        in_specs=[VMEM],
        out_specs=VMEM,
        compiler_params=params(32),
        name="finish",
    )(routed)


def solution(mesh):
    fine = Mesh(mesh.devices.reshape(NY, NCORE, NX, NZ), ("y", "core", "x", "z"))
    every = ("y", "core", "x", "z")
    in_specs = (P(every, None), P(every, None), P(), P(), P(every), P(("y", "core")), P())
    return jax.shard_map(body, mesh=fine, in_specs=in_specs, out_specs=P(every, None), check_vma=False)
```

```python
import jax
import jax.numpy as jnp
import numpy as np
from jax import lax
from jax.experimental import pallas as pl
from jax.experimental.pallas import tpu as pltpu
from jax.sharding import Mesh
from jax.sharding import PartitionSpec as P

MODEL_WIDTH = 4096
HIDDEN_UNITS = 14336
RANK = 16
SKETCH = 4096
BLOCKS = 32
TOK_DEV = 128
EXMAX = 4
EXAMPLES = 64
NY, NCORE, NX, NZ = 4, 2, 4, 8
CHIPS = NY * NX
COLS = (MODEL_WIDTH + HIDDEN_UNITS) // CHIPS
ROWS = EXMAX * RANK
LANES = 128
TILES = COLS // LANES
A_WIDTH = MODEL_WIDTH // BLOCKS
B_WIDTH = HIDDEN_UNITS // BLOCKS
PAIRS = RANK // 2
SLOTS = NCORE * CHIPS * EXMAX
KDEV = SKETCH // NCORE
KTILE = KDEV // NX
CUT_SLOTS = NX * EXMAX
PIECES = NCORE * KTILE // LANES
GROUPS = (3, 6, 9, 13, 16)
EARLY = PAIRS // 2


def as_i32(value):
    value &= 0xFFFFFFFF
    return np.int32(value - (1 << 32) if value >= 1 << 31 else value)


Q_STEP = 1640531527
K_STEP = 668265263
MULT = as_i32(739982445 << 11)
NT = (((1,), (1,)), ((), ()))
F32 = jnp.float32
BF16 = jnp.bfloat16
I32 = jnp.int32


def iota(shape, dim):
    return lax.broadcasted_iota(I32, shape, dim)


def gradient_kernel(
    tok_hbm, first_hbm, act_hbm, gout_hbm, down_hbm, up_hbm, out_hbm,
    tok_ref, first_ref, act_ref, gout_ref, down_ref, up_ref, made_ref, sems, sent,
):
    copies = [
        pltpu.make_async_copy(src, dst, sems.at[i])
        for i, (src, dst) in enumerate(
            (
                (down_hbm, down_ref),
                (act_hbm, act_ref),
                (tok_hbm, tok_ref),
                (first_hbm, first_ref),
                (up_hbm, up_ref),
            )
        )
    ]
    for lo, hi in zip(GROUPS[:-1], GROUPS[1:]):
        columns = slice(max(lo * COLS - MODEL_WIDTH, 0), hi * COLS - MODEL_WIDTH)
        copies.append(
            pltpu.make_async_copy(
                gout_hbm.at[:, columns], gout_ref.at[:, columns], sems.at[len(copies)]
            )
        )
    for copy in copies:
        copy.start()
    expand = (lax.rem(iota((ROWS, RANK), 0), RANK) == iota((ROWS, RANK), 1)).astype(F32).astype(BF16)
    for copy in copies[:4]:
        copy.wait()
    cut = lax.axis_index("x") * NZ + lax.axis_index("z")
    slot = tok_ref[...] - first_ref[cut]
    mine = (iota((ROWS, TOK_DEV), 0) // RANK) == slot

    def spread(factor):
        rows = lax.dot_general(expand, factor.astype(BF16), NT, preferred_element_type=F32)
        return jnp.where(mine, rows, 0.0).astype(BF16)

    spread_down = spread(
        lax.dot_general(act_ref[...], down_ref[...], NT, preferred_element_type=F32)
    )
    copies[4].wait()
    def send(chip):
        return pltpu.make_async_copy(made_ref.at[chip], out_hbm.at[chip], sent.at[chip])

    up = jnp.zeros((TOK_DEV, RANK), F32)
    for group, (first, last) in enumerate(zip(GROUPS[:-1], GROUPS[1:])):
        copies[5 + group].wait()
        for chip in range(first, last):
            lo, hi = max(chip * COLS - MODEL_WIDTH, 0), (chip + 1) * COLS - MODEL_WIDTH
            up = up + lax.dot_general(
                gout_ref[:, lo:hi], up_ref[:, lo:hi], NT, preferred_element_type=F32
            )
            part = jnp.dot(spread_down, gout_ref[:, lo:hi], preferred_element_type=F32)
            made_ref[chip, :, COLS - (hi - lo) :] = part.astype(BF16)
            if chip > GROUPS[0]:
                send(chip).start()
    spread_up = spread(up)
    for chip in range(GROUPS[0] + 1):
        lo, hi = chip * COLS, min((chip + 1) * COLS, MODEL_WIDTH)
        part = jnp.dot(spread_up, act_ref[:, lo:hi], preferred_element_type=F32)
        made_ref[chip, :, : hi - lo] = part.astype(BF16)
        send(chip).start()
    for chip in range(CHIPS):
        send(chip).wait()


def width_of(chip, tile):
    return jnp.where(chip * COLS + tile * LANES < MODEL_WIDTH, A_WIDTH, B_WIDTH)


def signs_of(base_ref, chip, p, feature):
    for half in range(2):
        for tile in range(TILES):
            shift = width_of(chip, tile) * (2 * p + half) * as_i32(Q_STEP)
            there = [
                feature + (as_i32(k * K_STEP) + shift) for k in range(0, KTILE, LANES)
            ]
            for row in range(tile * LANES, (tile + 1) * LANES, 16):
                base = base_ref[row : row + 16]
                signs = []
                for here in there:
                    h = base + here
                    h = (h ^ lax.shift_right_logical(h, np.int32(15))) * MULT
                    signs.append(jnp.where(h < 0, BF16(1), BF16(-1)))
                yield half * COLS + row, jnp.concatenate(signs, axis=1)


def first_feature(core, step):
    return (iota((16, LANES), 1) + (core * KDEV + step * KTILE)) * as_i32(K_STEP)


def sign_kernel(where_ref, seeds_ref, base_ref, sign_hbm, made_ref, sems):
    chip, core = where_ref[0], where_ref[1]
    row = iota((LANES, LANES), 0)
    for tile in range(TILES):
        column = chip * COLS + tile * LANES
        is_a = column < MODEL_WIDTH
        f = jnp.maximum(column - MODEL_WIDTH, 0)
        width = width_of(chip, tile)
        block = jnp.where(is_a, column // A_WIDTH, f // B_WIDTH)
        into = jnp.where(is_a, 0, f - f // B_WIDTH * B_WIDTH)
        after = jnp.minimum(block + 1, BLOCKS - 1)
        place = row + into
        over = place >= width
        seed = jnp.where(over, seeds_ref[after], seeds_ref[block])
        place = jnp.where(over, place - width, place)
        start = jnp.where(is_a, 0, RANK * A_WIDTH)
        base = (place + start) * as_i32(Q_STEP) + seed
        base_ref[tile * LANES : (tile + 1) * LANES] = base

    def send(i):
        slot = lax.rem(i, 2)
        return pltpu.make_async_copy(made_ref.at[slot], sign_hbm.at[i], sems.at[slot])

    def fill(i, carry):
        @pl.when(i >= 2)
        def _():
            send(i - 2).wait()

        slot = lax.rem(i, 2)
        tile, p = i // EARLY, lax.rem(i, EARLY)
        for row, signs in signs_of(base_ref, chip, p, first_feature(core, tile)):
            made_ref[slot, row : row + 16] = signs
        send(i).start()
        return carry

    lax.fori_loop(0, NX * EARLY, fill, 0)
    send(NX * EARLY - 2).wait()
    send(NX * EARLY - 1).wait()


def sketch_kernel(
    where_ref, base_ref, sign_hbm, own_ref, partner_ref, out_ref, vec_ref, acc_ref, sign_ref, sems
):
    chip, core = where_ref[0], where_ref[1]

    def fetch(i):
        slot = lax.rem(i, 3)
        return pltpu.make_async_copy(sign_hbm.at[i], sign_ref.at[slot], sems.at[slot])

    fetch(0).start()
    fetch(1).start()
    to, at = iota((256, 256), 0), iota((256, 256), 1)
    source = lax.rem(to, 16) // EXMAX * ROWS + lax.rem(to, EXMAX) * RANK + to // 16
    order = (at == source).astype(F32).astype(BF16)
    for half, ref in enumerate((own_ref, partner_ref)):
        for y in range(NY):
            rows = ref[NX * y : NX * (y + 1)].reshape(NX * ROWS, COLS)
            rows = jnp.dot(order, rows, preferred_element_type=F32).astype(BF16)
            lo = half * CHIPS * EXMAX + y * CUT_SLOTS
            for r in range(RANK):
                vec_ref[r // 2, lo : lo + CUT_SLOTS, (r % 2) * COLS : (r % 2 + 1) * COLS] = rows[
                    r * CUT_SLOTS : (r + 1) * CUT_SLOTS
                ]

    def tile(step, carry):
        feature = first_feature(core, step)
        acc_ref[...] = jnp.zeros_like(acc_ref)

        def pair(i, carry):
            n = step * EARLY + i

            @pl.when(n + 2 < NX * EARLY)
            def _():
                fetch(n + 2).start()

            fetch(n).wait()
            early = jnp.dot(vec_ref[i], sign_ref[lax.rem(n, 3)], preferred_element_type=F32)
            late = [signs for _, signs in signs_of(base_ref, chip, EARLY + i, feature)]
            late = jnp.concatenate(late, axis=0)
            late = jnp.dot(vec_ref[EARLY + i], late, preferred_element_type=F32)
            acc_ref[...] += early + late
            return carry

        lax.fori_loop(0, EARLY, pair, 0)
        total = acc_ref[...].astype(BF16)
        for half in range(NCORE):
            to_core = core if half == 0 else 1 - core
            for y in range(NY):
                lo = half * CHIPS * EXMAX + y * CUT_SLOTS
                out_ref[y, to_core, step] = total[lo : lo + CUT_SLOTS]
        return carry

    lax.fori_loop(0, NX, tile, 0)


def route_kernel(first_ref, z_ref, in_ref, out_ref):
    sums = []
    for c in range(NCORE):
        total = jnp.zeros((CUT_SLOTS, KTILE), F32)
        for y in range(NY):
            for x in range(NX):
                total = total + in_ref[(y * NCORE + c) * NX + x].astype(F32)
        sums.append(total.astype(BF16))
    stacked = jnp.concatenate(
        [
            sums[c][:, u * LANES : (u + 1) * LANES]
            for c in range(NCORE)
            for u in range(KTILE // LANES)
        ],
        axis=0,
    )
    z = z_ref[0]
    width = PIECES * CUT_SLOTS
    row, col = iota((EXAMPLES * PIECES, width), 0), iota((EXAMPLES * PIECES, width), 1)
    slot = lax.rem(col, CUT_SLOTS)
    example = jnp.full(row.shape, -1, I32)
    for x in range(NX):
        cut = x * NZ + z
        number = first_ref[cut] + lax.rem(slot, EXMAX)
        number = jnp.where(number < first_ref[cut + 1], number, -1)
        example = jnp.where(slot // EXMAX == x, number, example)
    hit = (row // PIECES == example) & (lax.rem(row, PIECES) == col // CUT_SLOTS)
    routed = jnp.dot(hit.astype(F32).astype(BF16), stacked, preferred_element_type=F32)
    out_ref[...] = routed.astype(BF16).reshape(out_ref.shape)


def finish_kernel(in_ref, out_ref):
    scale = float(RANK * (MODEL_WIDTH + HIDDEN_UNITS) * TOK_DEV) ** (-0.5)
    per = KTILE // LANES
    for x in range(NX):
        total = jnp.zeros(in_ref.shape[1:], F32)
        for z in range(NZ):
            total = total + in_ref[x * NZ + z].astype(F32)
        total = total * scale
        for p in range(2):
            for c in range(NCORE):
                for u in range(per):
                    row = p * PIECES + c * per + u
                    lo = c * KDEV + x * KTILE + u * LANES
                    out_ref[p : p + 1, lo : lo + LANES] = total[row : row + 1]


VMEM = pl.BlockSpec(memory_space=pltpu.VMEM)
SMEM = pl.BlockSpec(memory_space=pltpu.SMEM)
HBM = pl.BlockSpec(memory_space=pltpu.HBM)


def in_hbm(array):
    return pltpu.with_memory_space_constraint(array, pltpu.HBM)


def params(mib):
    return pltpu.CompilerParams(vmem_limit_bytes=mib << 20)


def body(acts, gouts, adapter_down, adapter_up, token_example, cut_first, seeds):
    y, core, x, z = (lax.axis_index(name) for name in ("y", "core", "x", "z"))
    grads = pl.pallas_call(
        gradient_kernel,
        out_shape=pltpu.HBM((CHIPS, ROWS, COLS), BF16),
        in_specs=[HBM] * 6,
        out_specs=HBM,
        scratch_shapes=[
            pltpu.VMEM((1, TOK_DEV), I32),
            pltpu.SMEM((cut_first.shape[0],), I32),
            pltpu.VMEM(acts.shape, BF16),
            pltpu.VMEM(gouts.shape, BF16),
            pltpu.VMEM((RANK, MODEL_WIDTH), BF16),
            pltpu.VMEM(adapter_up.shape, BF16),
            pltpu.VMEM((CHIPS, ROWS, COLS), BF16),
            pltpu.SemaphoreType.DMA((5 + len(GROUPS) - 1,)),
            pltpu.SemaphoreType.DMA((CHIPS,)),
        ],
        compiler_params=params(16),
        name="gradients",
    )(*(in_hbm(a) for a in (token_example.reshape(1, TOK_DEV), cut_first, acts, gouts, adapter_down.T, adapter_up)))
    where = jnp.stack([(y * NX + x).astype(I32), core.astype(I32)])
    where, seeds, grads = lax.optimization_barrier((where, seeds, grads))
    own = lax.all_to_all(grads, ("y", "x"), 0, 0, tiled=True)
    base, early = pl.pallas_call(
        sign_kernel,
        out_shape=(
            pltpu.VMEM((COLS, LANES), I32),
            pltpu.HBM((NX * EARLY, 2 * COLS, KTILE), BF16),
        ),
        in_specs=[SMEM, SMEM],
        out_specs=(VMEM, HBM),
        scratch_shapes=[
            pltpu.VMEM((2, 2 * COLS, KTILE), BF16),
            pltpu.SemaphoreType.DMA((2,)),
        ],
        cost_estimate=pl.CostEstimate(flops=20_000_000_000, bytes_accessed=0, transcendentals=0),
        compiler_params=params(16),
        name="signs",
    )(where, seeds)
    own, base = lax.optimization_barrier((own, base))
    partner = lax.ppermute(own, "core", [(0, 1), (1, 0)])
    parts = pl.pallas_call(
        sketch_kernel,
        out_shape=jax.ShapeDtypeStruct((NY, NCORE, NX, CUT_SLOTS, KTILE), BF16),
        in_specs=[SMEM, VMEM, HBM, VMEM, VMEM],
        out_specs=VMEM,
        scratch_shapes=[
            pltpu.VMEM((PAIRS, SLOTS, 2 * COLS), BF16),
            pltpu.VMEM((SLOTS, KTILE), F32),
            pltpu.VMEM((3, 2 * COLS, KTILE), BF16),
            pltpu.SemaphoreType.DMA((3,)),
        ],
        compiler_params=params(32),
        name="sketch",
    )(where, base, in_hbm(early), own, partner)
    parts = parts.reshape(NY * NCORE * NX, CUT_SLOTS, KTILE)
    parts = lax.all_to_all(parts, ("y", "core", "x"), 0, 0, tiled=True)
    routed = pl.pallas_call(
        route_kernel,
        out_shape=jax.ShapeDtypeStruct((NX * NZ, 2 * PIECES, LANES), BF16),
        in_specs=[SMEM, SMEM, VMEM],
        out_specs=VMEM,
        compiler_params=params(32),
        name="route",
    )(cut_first, z.astype(I32).reshape(1), parts)
    routed = lax.all_to_all(routed, ("x", "z"), 0, 0, tiled=True)
    return pl.pallas_call(
        finish_kernel,
        out_shape=jax.ShapeDtypeStruct((2, SKETCH), F32),
        in_specs=[VMEM],
        out_specs=VMEM,
        compiler_params=params(32),
        name="finish",
    )(routed)


def solution(mesh):
    fine = Mesh(mesh.devices.reshape(NY, NCORE, NX, NZ), ("y", "core", "x", "z"))
    every = ("y", "core", "x", "z")
    in_specs = (P(every, None), P(every, None), P(), P(), P(every), P(("y", "core")), P())
    return jax.shard_map(body, mesh=fine, in_specs=in_specs, out_specs=P(every, None), check_vma=False)
```

```python
import jax
import jax.numpy as jnp
import numpy as np
from jax import lax
from jax.experimental import pallas as pl
from jax.experimental.pallas import tpu as pltpu
from jax.sharding import Mesh
from jax.sharding import PartitionSpec as P

MODEL_WIDTH = 4096
HIDDEN_UNITS = 14336
RANK = 16
SKETCH = 4096
BLOCKS = 32
TOK_DEV = 128
EXMAX = 4
EXAMPLES = 64
NY, NCORE, NX, NZ = 4, 2, 4, 8
CHIPS = NY * NX
COLS = (MODEL_WIDTH + HIDDEN_UNITS) // CHIPS
ROWS = EXMAX * RANK
LANES = 128
TILES = COLS // LANES
A_WIDTH = MODEL_WIDTH // BLOCKS
B_WIDTH = HIDDEN_UNITS // BLOCKS
PAIRS = RANK // 2
SLOTS = NCORE * CHIPS * EXMAX
KDEV = SKETCH // NCORE
KTILE = KDEV // NX
CUT_SLOTS = NX * EXMAX
PIECES = NCORE * KTILE // LANES
GROUPS = (3, 6, 9, 13, 16)
DEPTH = 256
EARLY = PAIRS // 2


def as_i32(value):
    value &= 0xFFFFFFFF
    return np.int32(value - (1 << 32) if value >= 1 << 31 else value)


Q_STEP = 1640531527
K_STEP = 668265263
MULT = as_i32(739982445 << 11)
NT = (((1,), (1,)), ((), ()))
F32 = jnp.float32
BF16 = jnp.bfloat16
I32 = jnp.int32


def iota(shape, dim):
    return lax.broadcasted_iota(I32, shape, dim)


def gradient_kernel(
    tok_hbm, first_hbm, act_hbm, gout_hbm, down_hbm, up_hbm, out_hbm,
    tok_ref, first_ref, act_ref, gout_ref, down_ref, up_ref, made_ref, sems, sent,
):
    copies = [
        pltpu.make_async_copy(src, dst, sems.at[i])
        for i, (src, dst) in enumerate(
            (
                (down_hbm, down_ref),
                (act_hbm, act_ref),
                (tok_hbm, tok_ref),
                (first_hbm, first_ref),
                (up_hbm, up_ref),
            )
        )
    ]
    for lo, hi in zip(GROUPS[:-1], GROUPS[1:]):
        columns = slice(max(lo * COLS - MODEL_WIDTH, 0), hi * COLS - MODEL_WIDTH)
        copies.append(
            pltpu.make_async_copy(
                gout_hbm.at[:, columns], gout_ref.at[:, columns], sems.at[len(copies)]
            )
        )
    for copy in copies:
        copy.start()
    expand = (lax.rem(iota((ROWS, RANK), 0), RANK) == iota((ROWS, RANK), 1)).astype(F32).astype(BF16)
    for copy in copies[:4]:
        copy.wait()
    cut = lax.axis_index("x") * NZ + lax.axis_index("z")
    slot = tok_ref[...] - first_ref[cut]
    mine = (iota((ROWS, TOK_DEV), 0) // RANK) == slot

    def spread(factor):
        rows = lax.dot_general(expand, factor.astype(BF16), NT, preferred_element_type=F32)
        return jnp.where(mine, rows, 0.0).astype(BF16)

    spread_down = spread(
        lax.dot_general(act_ref[...], down_ref[...], NT, preferred_element_type=F32)
    )
    copies[4].wait()
    def send(chip):
        return pltpu.make_async_copy(made_ref.at[chip], out_hbm.at[chip], sent.at[chip])

    up = jnp.zeros((TOK_DEV, RANK), F32)
    for group, (first, last) in enumerate(zip(GROUPS[:-1], GROUPS[1:])):
        copies[5 + group].wait()
        for chip in range(first, last):
            lo, hi = max(chip * COLS - MODEL_WIDTH, 0), (chip + 1) * COLS - MODEL_WIDTH
            up = up + lax.dot_general(
                gout_ref[:, lo:hi], up_ref[:, lo:hi], NT, preferred_element_type=F32
            )
            part = jnp.dot(spread_down, gout_ref[:, lo:hi], preferred_element_type=F32)
            made_ref[chip, :, COLS - (hi - lo) :] = part.astype(BF16)
            if chip > GROUPS[0]:
                send(chip).start()
    spread_up = spread(up)
    for chip in range(GROUPS[0] + 1):
        lo, hi = chip * COLS, min((chip + 1) * COLS, MODEL_WIDTH)
        part = jnp.dot(spread_up, act_ref[:, lo:hi], preferred_element_type=F32)
        made_ref[chip, :, : hi - lo] = part.astype(BF16)
        send(chip).start()
    for chip in range(CHIPS):
        send(chip).wait()


def width_of(chip, tile):
    return jnp.where(chip * COLS + tile * LANES < MODEL_WIDTH, A_WIDTH, B_WIDTH)


def signs_of(base_ref, chip, p, feature):
    for half in range(2):
        for tile in range(TILES):
            shift = width_of(chip, tile) * (2 * p + half) * as_i32(Q_STEP)
            there = [
                feature + (as_i32(k * K_STEP) + shift) for k in range(0, KTILE, LANES)
            ]
            for row in range(tile * LANES, (tile + 1) * LANES, 16):
                base = base_ref[row : row + 16]
                signs = []
                for here in there:
                    h = base + here
                    h = (h ^ lax.shift_right_logical(h, np.int32(15))) * MULT
                    signs.append(jnp.where(h < 0, BF16(1), BF16(-1)))
                yield half * COLS + row, jnp.concatenate(signs, axis=1)


def first_feature(core, step):
    return (iota((16, LANES), 1) + (core * KDEV + step * KTILE)) * as_i32(K_STEP)


def sign_kernel(where_ref, seeds_ref, base_ref, sign_hbm, made_ref, sems):
    chip, core = where_ref[0], where_ref[1]
    row = iota((LANES, LANES), 0)
    for tile in range(TILES):
        column = chip * COLS + tile * LANES
        is_a = column < MODEL_WIDTH
        f = jnp.maximum(column - MODEL_WIDTH, 0)
        width = width_of(chip, tile)
        block = jnp.where(is_a, column // A_WIDTH, f // B_WIDTH)
        into = jnp.where(is_a, 0, f - f // B_WIDTH * B_WIDTH)
        after = jnp.minimum(block + 1, BLOCKS - 1)
        place = row + into
        over = place >= width
        seed = jnp.where(over, seeds_ref[after], seeds_ref[block])
        place = jnp.where(over, place - width, place)
        start = jnp.where(is_a, 0, RANK * A_WIDTH)
        base = (place + start) * as_i32(Q_STEP) + seed
        base_ref[tile * LANES : (tile + 1) * LANES] = base

    def send(i):
        slot = lax.rem(i, 2)
        return pltpu.make_async_copy(made_ref.at[slot], sign_hbm.at[i], sems.at[slot])

    def fill(i, carry):
        @pl.when(i >= 2)
        def _():
            send(i - 2).wait()

        slot = lax.rem(i, 2)
        tile, p = i // EARLY, lax.rem(i, EARLY)
        for row, signs in signs_of(base_ref, chip, p, first_feature(core, tile)):
            made_ref[slot, row : row + 16] = signs
        send(i).start()
        return carry

    lax.fori_loop(0, NX * EARLY, fill, 0)
    send(NX * EARLY - 2).wait()
    send(NX * EARLY - 1).wait()


def arrange(ref, vec_ref):
    to, at = iota((256, 256), 0), iota((256, 256), 1)
    source = lax.rem(to, 16) // EXMAX * ROWS + lax.rem(to, EXMAX) * RANK + to // 16
    order = (at == source).astype(F32).astype(BF16)
    for y in range(NY):
        rows = ref[NX * y : NX * (y + 1)].reshape(NX * ROWS, COLS)
        rows = jnp.dot(order, rows, preferred_element_type=F32).astype(BF16)
        lo = y * CUT_SLOTS
        for r in range(RANK):
            vec_ref[r // 2, lo : lo + CUT_SLOTS, (r % 2) * COLS : (r % 2 + 1) * COLS] = rows[
                r * CUT_SLOTS : (r + 1) * CUT_SLOTS
            ]


def arrange_kernel(in_ref, out_ref):
    arrange(in_ref, out_ref)


def sketch_kernel(
    where_ref, base_ref, sign_hbm, mine_ref, partner_ref, out_ref, vec_ref, acc_ref, sign_ref, sems
):
    chip, core = where_ref[0], where_ref[1]

    def fetch(i):
        slot = lax.rem(i, 2 * EARLY)
        return pltpu.make_async_copy(sign_hbm.at[i], sign_ref.at[slot], sems.at[slot])

    for i in range(EARLY):
        fetch(i).start()
    arrange(partner_ref, vec_ref)

    def vectors(p, q):
        return jnp.concatenate(
            [mine_ref[p, :, q : q + DEPTH], vec_ref[p, :, q : q + DEPTH]], axis=0
        )

    def tile(step, carry):
        feature = first_feature(core, step)
        acc_ref[...] = jnp.zeros_like(acc_ref)

        @pl.when(step + 1 < NX)
        def _():
            for i in range(EARLY):
                fetch((step + 1) * EARLY + i).start()

        def pair(i, carry):
            n = step * EARLY + i
            slot = lax.rem(n, 2 * EARLY)
            fetch(n).wait()
            made = signs_of(base_ref, chip, EARLY + i, feature)
            for q in range(0, 2 * COLS, DEPTH):
                late = jnp.concatenate([next(made)[1] for _ in range(DEPTH // 16)], axis=0)
                acc_ref[...] += jnp.dot(
                    vectors(i, q), sign_ref[slot, q : q + DEPTH], preferred_element_type=F32
                ) + jnp.dot(vectors(EARLY + i, q), late, preferred_element_type=F32)
            return carry

        lax.fori_loop(0, EARLY, pair, 0, unroll=True)
        total = acc_ref[...].astype(BF16)
        for half in range(NCORE):
            to_core = core if half == 0 else 1 - core
            for y in range(NY):
                lo = half * CHIPS * EXMAX + y * CUT_SLOTS
                out_ref[y, to_core, step] = total[lo : lo + CUT_SLOTS]
        return carry

    lax.fori_loop(0, NX, tile, 0)


def route_kernel(first_ref, z_ref, in_ref, out_ref):
    sums = []
    for c in range(NCORE):
        total = jnp.zeros((CUT_SLOTS, KTILE), F32)
        for y in range(NY):
            for x in range(NX):
                total = total + in_ref[(y * NCORE + c) * NX + x].astype(F32)
        sums.append(total.astype(BF16))
    stacked = jnp.concatenate(
        [
            sums[c][:, u * LANES : (u + 1) * LANES]
            for c in range(NCORE)
            for u in range(KTILE // LANES)
        ],
        axis=0,
    )
    z = z_ref[0]
    width = PIECES * CUT_SLOTS
    row, col = iota((EXAMPLES * PIECES, width), 0), iota((EXAMPLES * PIECES, width), 1)
    slot = lax.rem(col, CUT_SLOTS)
    example = jnp.full(row.shape, -1, I32)
    for x in range(NX):
        cut = x * NZ + z
        number = first_ref[cut] + lax.rem(slot, EXMAX)
        number = jnp.where(number < first_ref[cut + 1], number, -1)
        example = jnp.where(slot // EXMAX == x, number, example)
    hit = (row // PIECES == example) & (lax.rem(row, PIECES) == col // CUT_SLOTS)
    routed = jnp.dot(hit.astype(F32).astype(BF16), stacked, preferred_element_type=F32)
    out_ref[...] = routed.astype(BF16).reshape(out_ref.shape)


def finish_kernel(in_ref, out_ref):
    scale = float(RANK * (MODEL_WIDTH + HIDDEN_UNITS) * TOK_DEV) ** (-0.5)
    per = KTILE // LANES
    for x in range(NX):
        total = jnp.zeros(in_ref.shape[1:], F32)
        for z in range(NZ):
            total = total + in_ref[x * NZ + z].astype(F32)
        total = total * scale
        for p in range(2):
            for c in range(NCORE):
                for u in range(per):
                    row = p * PIECES + c * per + u
                    lo = c * KDEV + x * KTILE + u * LANES
                    out_ref[p : p + 1, lo : lo + LANES] = total[row : row + 1]


VMEM = pl.BlockSpec(memory_space=pltpu.VMEM)
SMEM = pl.BlockSpec(memory_space=pltpu.SMEM)
HBM = pl.BlockSpec(memory_space=pltpu.HBM)


def in_hbm(array):
    return pltpu.with_memory_space_constraint(array, pltpu.HBM)


def params(mib):
    return pltpu.CompilerParams(vmem_limit_bytes=mib << 20)


def body(acts, gouts, adapter_down, adapter_up, token_example, cut_first, seeds):
    y, core, x, z = (lax.axis_index(name) for name in ("y", "core", "x", "z"))
    grads = pl.pallas_call(
        gradient_kernel,
        out_shape=pltpu.HBM((CHIPS, ROWS, COLS), BF16),
        in_specs=[HBM] * 6,
        out_specs=HBM,
        scratch_shapes=[
            pltpu.VMEM((1, TOK_DEV), I32),
            pltpu.SMEM((cut_first.shape[0],), I32),
            pltpu.VMEM(acts.shape, BF16),
            pltpu.VMEM(gouts.shape, BF16),
            pltpu.VMEM((RANK, MODEL_WIDTH), BF16),
            pltpu.VMEM(adapter_up.shape, BF16),
            pltpu.VMEM((CHIPS, ROWS, COLS), BF16),
            pltpu.SemaphoreType.DMA((5 + len(GROUPS) - 1,)),
            pltpu.SemaphoreType.DMA((CHIPS,)),
        ],
        compiler_params=params(16),
        name="gradients",
    )(*(in_hbm(a) for a in (token_example.reshape(1, TOK_DEV), cut_first, acts, gouts, adapter_down.T, adapter_up)))
    where = jnp.stack([(y * NX + x).astype(I32), core.astype(I32)])
    where, seeds, grads = lax.optimization_barrier((where, seeds, grads))
    own = lax.all_to_all(grads, ("y", "x"), 0, 0, tiled=True)
    base, early = pl.pallas_call(
        sign_kernel,
        out_shape=(
            pltpu.VMEM((COLS, LANES), I32),
            pltpu.HBM((NX * EARLY, 2 * COLS, KTILE), BF16),
        ),
        in_specs=[SMEM, SMEM],
        out_specs=(VMEM, HBM),
        scratch_shapes=[
            pltpu.VMEM((2, 2 * COLS, KTILE), BF16),
            pltpu.SemaphoreType.DMA((2,)),
        ],
        cost_estimate=pl.CostEstimate(flops=20_000_000_000, bytes_accessed=0, transcendentals=0),
        compiler_params=params(16),
        name="signs",
    )(where, seeds)
    own, base = lax.optimization_barrier((own, base))
    partner = lax.ppermute(own, "core", [(0, 1), (1, 0)])
    mine = pl.pallas_call(
        arrange_kernel,
        out_shape=jax.ShapeDtypeStruct((PAIRS, SLOTS // NCORE, 2 * COLS), BF16),
        in_specs=[VMEM],
        out_specs=VMEM,
        cost_estimate=pl.CostEstimate(flops=1_500_000_000, bytes_accessed=0, transcendentals=0),
        compiler_params=params(16),
        name="arrange",
    )(own)
    parts = pl.pallas_call(
        sketch_kernel,
        out_shape=jax.ShapeDtypeStruct((NY, NCORE, NX, CUT_SLOTS, KTILE), BF16),
        in_specs=[SMEM, VMEM, HBM, VMEM, VMEM],
        out_specs=VMEM,
        scratch_shapes=[
            pltpu.VMEM((PAIRS, SLOTS // NCORE, 2 * COLS), BF16),
            pltpu.VMEM((SLOTS, KTILE), F32),
            pltpu.VMEM((2 * EARLY, 2 * COLS, KTILE), BF16),
            pltpu.SemaphoreType.DMA((2 * EARLY,)),
        ],
        compiler_params=params(32),
        name="sketch",
    )(where, base, in_hbm(early), mine, partner)
    parts = parts.reshape(NY * NCORE * NX, CUT_SLOTS, KTILE)
    parts = lax.all_to_all(parts, ("y", "core", "x"), 0, 0, tiled=True)
    routed = pl.pallas_call(
        route_kernel,
        out_shape=jax.ShapeDtypeStruct((NX * NZ, 2 * PIECES, LANES), BF16),
        in_specs=[SMEM, SMEM, VMEM],
        out_specs=VMEM,
        compiler_params=params(32),
        name="route",
    )(cut_first, z.astype(I32).reshape(1), parts)
    routed = lax.all_to_all(routed, ("x", "z"), 0, 0, tiled=True)
    return pl.pallas_call(
        finish_kernel,
        out_shape=jax.ShapeDtypeStruct((2, SKETCH), F32),
        in_specs=[VMEM],
        out_specs=VMEM,
        compiler_params=params(32),
        name="finish",
    )(routed)


def solution(mesh):
    fine = Mesh(mesh.devices.reshape(NY, NCORE, NX, NZ), ("y", "core", "x", "z"))
    every = ("y", "core", "x", "z")
    in_specs = (P(every, None), P(every, None), P(), P(), P(every), P(("y", "core")), P())
    return jax.shard_map(body, mesh=fine, in_specs=in_specs, out_specs=P(every, None), check_vma=False)
```

```python
import jax
import jax.numpy as jnp
import numpy as np
from jax import lax
from jax.experimental import pallas as pl
from jax.experimental.pallas import tpu as pltpu
from jax.sharding import Mesh
from jax.sharding import PartitionSpec as P

MODEL_WIDTH = 4096
HIDDEN_UNITS = 14336
RANK = 16
SKETCH = 4096
BLOCKS = 32
TOK_DEV = 128
EXMAX = 4
EXAMPLES = 64
NY, NCORE, NX, NZ = 4, 2, 4, 8
CHIPS = NY * NX
COLS = (MODEL_WIDTH + HIDDEN_UNITS) // CHIPS
ROWS = EXMAX * RANK
LANES = 128
TILES = COLS // LANES
A_WIDTH = MODEL_WIDTH // BLOCKS
B_WIDTH = HIDDEN_UNITS // BLOCKS
PAIRS = RANK // 2
SLOTS = NCORE * CHIPS * EXMAX
KDEV = SKETCH // NCORE
KTILE = KDEV // NX
CUT_SLOTS = NX * EXMAX
PIECES = NCORE * KTILE // LANES
GROUPS = (3, 6, 9, 13, 16)
DEPTH = 256
EARLY = 5


def as_i32(value):
    value &= 0xFFFFFFFF
    return np.int32(value - (1 << 32) if value >= 1 << 31 else value)


Q_STEP = 1640531527
K_STEP = 668265263
MULT = as_i32(739982445 << 11)
NT = (((1,), (1,)), ((), ()))
F32 = jnp.float32
BF16 = jnp.bfloat16
I32 = jnp.int32


def iota(shape, dim):
    return lax.broadcasted_iota(I32, shape, dim)


def gradient_kernel(
    tok_hbm, first_hbm, act_hbm, gout_hbm, down_hbm, up_hbm, out_hbm,
    tok_ref, first_ref, act_ref, gout_ref, down_ref, up_ref, made_ref, sems, sent,
):
    copies = [
        pltpu.make_async_copy(src, dst, sems.at[i])
        for i, (src, dst) in enumerate(
            (
                (down_hbm, down_ref),
                (act_hbm, act_ref),
                (tok_hbm, tok_ref),
                (first_hbm, first_ref),
                (up_hbm, up_ref),
            )
        )
    ]
    for lo, hi in zip(GROUPS[:-1], GROUPS[1:]):
        columns = slice(max(lo * COLS - MODEL_WIDTH, 0), hi * COLS - MODEL_WIDTH)
        copies.append(
            pltpu.make_async_copy(
                gout_hbm.at[:, columns], gout_ref.at[:, columns], sems.at[len(copies)]
            )
        )
    for copy in copies:
        copy.start()
    expand = (lax.rem(iota((ROWS, RANK), 0), RANK) == iota((ROWS, RANK), 1)).astype(F32).astype(BF16)
    for copy in copies[:4]:
        copy.wait()
    cut = lax.axis_index("x") * NZ + lax.axis_index("z")
    slot = tok_ref[...] - first_ref[cut]
    mine = (iota((ROWS, TOK_DEV), 0) // RANK) == slot

    def spread(factor):
        rows = lax.dot_general(expand, factor.astype(BF16), NT, preferred_element_type=F32)
        return jnp.where(mine, rows, 0.0).astype(BF16)

    spread_down = spread(
        lax.dot_general(act_ref[...], down_ref[...], NT, preferred_element_type=F32)
    )
    copies[4].wait()
    def send(chip):
        return pltpu.make_async_copy(made_ref.at[chip], out_hbm.at[chip], sent.at[chip])

    up = jnp.zeros((TOK_DEV, RANK), F32)
    for group, (first, last) in enumerate(zip(GROUPS[:-1], GROUPS[1:])):
        copies[5 + group].wait()
        for chip in range(first, last):
            lo, hi = max(chip * COLS - MODEL_WIDTH, 0), (chip + 1) * COLS - MODEL_WIDTH
            up = up + lax.dot_general(
                gout_ref[:, lo:hi], up_ref[:, lo:hi], NT, preferred_element_type=F32
            )
            part = jnp.dot(spread_down, gout_ref[:, lo:hi], preferred_element_type=F32)
            made_ref[chip, :, COLS - (hi - lo) :] = part.astype(BF16)
            if chip > GROUPS[0]:
                send(chip).start()
    spread_up = spread(up)
    for chip in range(GROUPS[0] + 1):
        lo, hi = chip * COLS, min((chip + 1) * COLS, MODEL_WIDTH)
        part = jnp.dot(spread_up, act_ref[:, lo:hi], preferred_element_type=F32)
        made_ref[chip, :, : hi - lo] = part.astype(BF16)
        send(chip).start()
    for chip in range(CHIPS):
        send(chip).wait()


def width_of(chip, tile):
    return jnp.where(chip * COLS + tile * LANES < MODEL_WIDTH, A_WIDTH, B_WIDTH)


def signs_of(base_ref, chip, p, feature):
    for half in range(2):
        for tile in range(TILES):
            shift = width_of(chip, tile) * (2 * p + half) * as_i32(Q_STEP)
            there = [
                feature + (as_i32(k * K_STEP) + shift) for k in range(0, KTILE, LANES)
            ]
            for row in range(tile * LANES, (tile + 1) * LANES, 16):
                base = base_ref[row : row + 16]
                signs = []
                for here in there:
                    h = base + here
                    h = (h ^ lax.shift_right_logical(h, np.int32(15))) * MULT
                    signs.append(jnp.where(h < 0, BF16(1), BF16(-1)))
                yield half * COLS + row, jnp.concatenate(signs, axis=1)


def first_feature(core, step):
    return (iota((16, LANES), 1) + (core * KDEV + step * KTILE)) * as_i32(K_STEP)


def sign_kernel(where_ref, seeds_ref, base_ref, sign_hbm, made_ref, sems):
    chip, core = where_ref[0], where_ref[1]
    row = iota((LANES, LANES), 0)
    for tile in range(TILES):
        column = chip * COLS + tile * LANES
        is_a = column < MODEL_WIDTH
        f = jnp.maximum(column - MODEL_WIDTH, 0)
        width = width_of(chip, tile)
        block = jnp.where(is_a, column // A_WIDTH, f // B_WIDTH)
        into = jnp.where(is_a, 0, f - f // B_WIDTH * B_WIDTH)
        after = jnp.minimum(block + 1, BLOCKS - 1)
        place = row + into
        over = place >= width
        seed = jnp.where(over, seeds_ref[after], seeds_ref[block])
        place = jnp.where(over, place - width, place)
        start = jnp.where(is_a, 0, RANK * A_WIDTH)
        base = (place + start) * as_i32(Q_STEP) + seed
        base_ref[tile * LANES : (tile + 1) * LANES] = base

    def send(i):
        slot = lax.rem(i, 2)
        return pltpu.make_async_copy(made_ref.at[slot], sign_hbm.at[i], sems.at[slot])

    def fill(i, carry):
        @pl.when(i >= 2)
        def _():
            send(i - 2).wait()

        slot = lax.rem(i, 2)
        tile, p = i // EARLY, lax.rem(i, EARLY)
        for row, signs in signs_of(base_ref, chip, p, first_feature(core, tile)):
            made_ref[slot, row : row + 16] = signs
        send(i).start()
        return carry

    lax.fori_loop(0, NX * EARLY, fill, 0)
    send(NX * EARLY - 2).wait()
    send(NX * EARLY - 1).wait()


def arrange(ref, vec_ref):
    to, at = iota((256, 256), 0), iota((256, 256), 1)
    source = lax.rem(to, 16) // EXMAX * ROWS + lax.rem(to, EXMAX) * RANK + to // 16
    order = (at == source).astype(F32).astype(BF16)
    for y in range(NY):
        rows = ref[NX * y : NX * (y + 1)].reshape(NX * ROWS, COLS)
        rows = jnp.dot(order, rows, preferred_element_type=F32).astype(BF16)
        lo = y * CUT_SLOTS
        for r in range(RANK):
            vec_ref[r // 2, lo : lo + CUT_SLOTS, (r % 2) * COLS : (r % 2 + 1) * COLS] = rows[
                r * CUT_SLOTS : (r + 1) * CUT_SLOTS
            ]


def arrange_kernel(in_ref, out_ref):
    arrange(in_ref, out_ref)


def sketch_kernel(
    where_ref, base_ref, sign_hbm, mine_ref, partner_ref, out_ref, vec_ref, acc_ref, sign_ref, sems
):
    chip, core = where_ref[0], where_ref[1]

    def fetch(i):
        slot = lax.rem(i, 2 * EARLY)
        return pltpu.make_async_copy(sign_hbm.at[i], sign_ref.at[slot], sems.at[slot])

    for i in range(EARLY):
        fetch(i).start()
    arrange(partner_ref, vec_ref)

    def vectors(p, q):
        return jnp.concatenate(
            [mine_ref[p, :, q : q + DEPTH], vec_ref[p, :, q : q + DEPTH]], axis=0
        )

    def tile(step, carry):
        feature = first_feature(core, step)
        acc_ref[...] = jnp.zeros_like(acc_ref)

        @pl.when(step + 1 < NX)
        def _():
            for i in range(EARLY):
                fetch((step + 1) * EARLY + i).start()

        chunks = range(0, 2 * COLS, DEPTH)
        stored = [(p, q) for p in range(EARLY) for q in chunks]
        fresh = [(p, q) for p in range(EARLY, PAIRS) for q in chunks]
        made = iter(())
        for j, (p, q) in enumerate(fresh):
            if q == 0:
                made = signs_of(base_ref, chip, p, feature)
            late = jnp.concatenate([next(made)[1] for _ in range(DEPTH // 16)], axis=0)
            sums = jnp.dot(vectors(p, q), late, preferred_element_type=F32)
            for e, at in stored[j * len(stored) // len(fresh) : (j + 1) * len(stored) // len(fresh)]:
                n = step * EARLY + e
                if at == 0:
                    fetch(n).wait()
                signs = sign_ref[lax.rem(n, 2 * EARLY), at : at + DEPTH].astype(BF16)
                sums = sums + jnp.dot(vectors(e, at), signs, preferred_element_type=F32)
            acc_ref[...] += sums
        total = acc_ref[...].astype(BF16)
        for half in range(NCORE):
            to_core = core if half == 0 else 1 - core
            for y in range(NY):
                lo = half * CHIPS * EXMAX + y * CUT_SLOTS
                out_ref[y, to_core, step] = total[lo : lo + CUT_SLOTS]
        return carry

    lax.fori_loop(0, NX, tile, 0)


def route_kernel(first_ref, z_ref, in_ref, out_ref):
    sums = []
    for c in range(NCORE):
        total = jnp.zeros((CUT_SLOTS, KTILE), F32)
        for y in range(NY):
            for x in range(NX):
                total = total + in_ref[(y * NCORE + c) * NX + x].astype(F32)
        sums.append(total.astype(BF16))
    stacked = jnp.concatenate(
        [
            sums[c][:, u * LANES : (u + 1) * LANES]
            for c in range(NCORE)
            for u in range(KTILE // LANES)
        ],
        axis=0,
    )
    z = z_ref[0]
    width = PIECES * CUT_SLOTS
    row, col = iota((EXAMPLES * PIECES, width), 0), iota((EXAMPLES * PIECES, width), 1)
    slot = lax.rem(col, CUT_SLOTS)
    example = jnp.full(row.shape, -1, I32)
    for x in range(NX):
        cut = x * NZ + z
        number = first_ref[cut] + lax.rem(slot, EXMAX)
        number = jnp.where(number < first_ref[cut + 1], number, -1)
        example = jnp.where(slot // EXMAX == x, number, example)
    hit = (row // PIECES == example) & (lax.rem(row, PIECES) == col // CUT_SLOTS)
    routed = jnp.dot(hit.astype(F32).astype(BF16), stacked, preferred_element_type=F32)
    out_ref[...] = routed.astype(BF16).reshape(out_ref.shape)


def finish_kernel(in_ref, out_ref):
    scale = float(RANK * (MODEL_WIDTH + HIDDEN_UNITS) * TOK_DEV) ** (-0.5)
    per = KTILE // LANES
    for x in range(NX):
        total = jnp.zeros(in_ref.shape[1:], F32)
        for z in range(NZ):
            total = total + in_ref[x * NZ + z].astype(F32)
        total = total * scale
        for p in range(2):
            for c in range(NCORE):
                for u in range(per):
                    row = p * PIECES + c * per + u
                    lo = c * KDEV + x * KTILE + u * LANES
                    out_ref[p : p + 1, lo : lo + LANES] = total[row : row + 1]


VMEM = pl.BlockSpec(memory_space=pltpu.VMEM)
SMEM = pl.BlockSpec(memory_space=pltpu.SMEM)
HBM = pl.BlockSpec(memory_space=pltpu.HBM)


def in_hbm(array):
    return pltpu.with_memory_space_constraint(array, pltpu.HBM)


def params(mib):
    return pltpu.CompilerParams(vmem_limit_bytes=mib << 20)


def body(acts, gouts, adapter_down, adapter_up, token_example, cut_first, seeds):
    y, core, x, z = (lax.axis_index(name) for name in ("y", "core", "x", "z"))
    grads = pl.pallas_call(
        gradient_kernel,
        out_shape=pltpu.HBM((CHIPS, ROWS, COLS), BF16),
        in_specs=[HBM] * 6,
        out_specs=HBM,
        scratch_shapes=[
            pltpu.VMEM((1, TOK_DEV), I32),
            pltpu.SMEM((cut_first.shape[0],), I32),
            pltpu.VMEM(acts.shape, BF16),
            pltpu.VMEM(gouts.shape, BF16),
            pltpu.VMEM((RANK, MODEL_WIDTH), BF16),
            pltpu.VMEM(adapter_up.shape, BF16),
            pltpu.VMEM((CHIPS, ROWS, COLS), BF16),
            pltpu.SemaphoreType.DMA((5 + len(GROUPS) - 1,)),
            pltpu.SemaphoreType.DMA((CHIPS,)),
        ],
        compiler_params=params(16),
        name="gradients",
    )(*(in_hbm(a) for a in (token_example.reshape(1, TOK_DEV), cut_first, acts, gouts, adapter_down.T, adapter_up)))
    where = jnp.stack([(y * NX + x).astype(I32), core.astype(I32)])
    where, seeds, grads = lax.optimization_barrier((where, seeds, grads))
    own = lax.all_to_all(grads, ("y", "x"), 0, 0, tiled=True)
    base, early = pl.pallas_call(
        sign_kernel,
        out_shape=(
            pltpu.VMEM((COLS, LANES), I32),
            pltpu.HBM((NX * EARLY, 2 * COLS, KTILE), BF16),
        ),
        in_specs=[SMEM, SMEM],
        out_specs=(VMEM, HBM),
        scratch_shapes=[
            pltpu.VMEM((2, 2 * COLS, KTILE), BF16),
            pltpu.SemaphoreType.DMA((2,)),
        ],
        cost_estimate=pl.CostEstimate(flops=20_000_000_000, bytes_accessed=0, transcendentals=0),
        compiler_params=params(16),
        name="signs",
    )(where, seeds)
    own, base = lax.optimization_barrier((own, base))
    partner = lax.ppermute(own, "core", [(0, 1), (1, 0)])
    mine = pl.pallas_call(
        arrange_kernel,
        out_shape=jax.ShapeDtypeStruct((PAIRS, SLOTS // NCORE, 2 * COLS), BF16),
        in_specs=[VMEM],
        out_specs=VMEM,
        cost_estimate=pl.CostEstimate(flops=1_500_000_000, bytes_accessed=0, transcendentals=0),
        compiler_params=params(16),
        name="arrange",
    )(own)
    parts = pl.pallas_call(
        sketch_kernel,
        out_shape=jax.ShapeDtypeStruct((NY, NCORE, NX, CUT_SLOTS, KTILE), BF16),
        in_specs=[SMEM, VMEM, HBM, VMEM, VMEM],
        out_specs=VMEM,
        scratch_shapes=[
            pltpu.VMEM((PAIRS, SLOTS // NCORE, 2 * COLS), BF16),
            pltpu.VMEM((SLOTS, KTILE), F32),
            pltpu.VMEM((2 * EARLY, 2 * COLS, KTILE), BF16),
            pltpu.SemaphoreType.DMA((2 * EARLY,)),
        ],
        compiler_params=params(40),
        name="sketch",
    )(where, base, in_hbm(early), mine, partner)
    parts = parts.reshape(NY * NCORE * NX, CUT_SLOTS, KTILE)
    parts = lax.all_to_all(parts, ("y", "core", "x"), 0, 0, tiled=True)
    routed = pl.pallas_call(
        route_kernel,
        out_shape=jax.ShapeDtypeStruct((NX * NZ, 2 * PIECES, LANES), BF16),
        in_specs=[SMEM, SMEM, VMEM],
        out_specs=VMEM,
        compiler_params=params(32),
        name="route",
    )(cut_first, z.astype(I32).reshape(1), parts)
    routed = lax.all_to_all(routed, ("x", "z"), 0, 0, tiled=True)
    return pl.pallas_call(
        finish_kernel,
        out_shape=jax.ShapeDtypeStruct((2, SKETCH), F32),
        in_specs=[VMEM],
        out_specs=VMEM,
        compiler_params=params(32),
        name="finish",
    )(routed)


def solution(mesh):
    fine = Mesh(mesh.devices.reshape(NY, NCORE, NX, NZ), ("y", "core", "x", "z"))
    every = ("y", "core", "x", "z")
    in_specs = (P(every, None), P(every, None), P(), P(), P(every), P(("y", "core")), P())
    return jax.shard_map(body, mesh=fine, in_specs=in_specs, out_specs=P(every, None), check_vma=False)
```

```python
import jax
import jax.numpy as jnp
import numpy as np
from jax import lax
from jax.experimental import pallas as pl
from jax.experimental.pallas import tpu as pltpu
from jax.sharding import Mesh
from jax.sharding import PartitionSpec as P

MODEL_WIDTH = 4096
HIDDEN_UNITS = 14336
RANK = 16
SKETCH = 4096
BLOCKS = 32
TOK_DEV = 128
EXMAX = 4
EXAMPLES = 64
NY, NCORE, NX, NZ = 4, 2, 4, 8
CHIPS = NY * NX
COLS = (MODEL_WIDTH + HIDDEN_UNITS) // CHIPS
ROWS = EXMAX * RANK
LANES = 128
TILES = COLS // LANES
A_WIDTH = MODEL_WIDTH // BLOCKS
B_WIDTH = HIDDEN_UNITS // BLOCKS
PAIRS = RANK // 2
SLOTS = NCORE * CHIPS * EXMAX
KDEV = SKETCH // NCORE
KTILE = KDEV // NX
CUT_SLOTS = NX * EXMAX
PIECES = NCORE * KTILE // LANES
GROUPS = (3, 6, 9, 13, 16)
DEPTH = 256
EARLY = 7


def as_i32(value):
    value &= 0xFFFFFFFF
    return np.int32(value - (1 << 32) if value >= 1 << 31 else value)


Q_STEP = 1640531527
K_STEP = 668265263
MULT = as_i32(739982445 << 11)
NT = (((1,), (1,)), ((), ()))
F32 = jnp.float32
BF16 = jnp.bfloat16
I32 = jnp.int32
F8 = jnp.float8_e4m3fn


def iota(shape, dim):
    return lax.broadcasted_iota(I32, shape, dim)


def gradient_kernel(
    tok_hbm, first_hbm, act_hbm, gout_hbm, down_hbm, up_hbm, out_hbm,
    tok_ref, first_ref, act_ref, gout_ref, down_ref, up_ref, made_ref, sems, sent,
):
    copies = [
        pltpu.make_async_copy(src, dst, sems.at[i])
        for i, (src, dst) in enumerate(
            (
                (down_hbm, down_ref),
                (act_hbm, act_ref),
                (tok_hbm, tok_ref),
                (first_hbm, first_ref),
                (up_hbm, up_ref),
            )
        )
    ]
    for lo, hi in zip(GROUPS[:-1], GROUPS[1:]):
        columns = slice(max(lo * COLS - MODEL_WIDTH, 0), hi * COLS - MODEL_WIDTH)
        copies.append(
            pltpu.make_async_copy(
                gout_hbm.at[:, columns], gout_ref.at[:, columns], sems.at[len(copies)]
            )
        )
    for copy in copies:
        copy.start()
    expand = (lax.rem(iota((ROWS, RANK), 0), RANK) == iota((ROWS, RANK), 1)).astype(F32).astype(BF16)
    for copy in copies[:4]:
        copy.wait()
    cut = lax.axis_index("x") * NZ + lax.axis_index("z")
    slot = tok_ref[...] - first_ref[cut]
    mine = (iota((ROWS, TOK_DEV), 0) // RANK) == slot

    def spread(factor):
        rows = lax.dot_general(expand, factor.astype(BF16), NT, preferred_element_type=F32)
        return jnp.where(mine, rows, 0.0).astype(BF16)

    spread_down = spread(
        lax.dot_general(act_ref[...], down_ref[...], NT, preferred_element_type=F32)
    )
    copies[4].wait()
    def send(chip):
        return pltpu.make_async_copy(made_ref.at[chip], out_hbm.at[chip], sent.at[chip])

    up = jnp.zeros((TOK_DEV, RANK), F32)
    for group, (first, last) in enumerate(zip(GROUPS[:-1], GROUPS[1:])):
        copies[5 + group].wait()
        for chip in range(first, last):
            lo, hi = max(chip * COLS - MODEL_WIDTH, 0), (chip + 1) * COLS - MODEL_WIDTH
            up = up + lax.dot_general(
                gout_ref[:, lo:hi], up_ref[:, lo:hi], NT, preferred_element_type=F32
            )
            part = jnp.dot(spread_down, gout_ref[:, lo:hi], preferred_element_type=F32)
            made_ref[chip, :, COLS - (hi - lo) :] = part.astype(BF16)
            if chip > GROUPS[0]:
                send(chip).start()
    spread_up = spread(up)
    for chip in range(GROUPS[0] + 1):
        lo, hi = chip * COLS, min((chip + 1) * COLS, MODEL_WIDTH)
        part = jnp.dot(spread_up, act_ref[:, lo:hi], preferred_element_type=F32)
        made_ref[chip, :, : hi - lo] = part.astype(BF16)
        send(chip).start()
    for chip in range(CHIPS):
        send(chip).wait()


def width_of(chip, tile):
    return jnp.where(chip * COLS + tile * LANES < MODEL_WIDTH, A_WIDTH, B_WIDTH)


def signs_of(base_ref, chip, p, feature):
    for half in range(2):
        for tile in range(TILES):
            shift = width_of(chip, tile) * (2 * p + half) * as_i32(Q_STEP)
            there = [
                feature + (as_i32(k * K_STEP) + shift) for k in range(0, KTILE, LANES)
            ]
            for row in range(tile * LANES, (tile + 1) * LANES, 16):
                base = base_ref[row : row + 16]
                signs = []
                for here in there:
                    h = base + here
                    h = (h ^ lax.shift_right_logical(h, np.int32(15))) * MULT
                    signs.append(jnp.where(h < 0, BF16(1), BF16(-1)))
                yield half * COLS + row, jnp.concatenate(signs, axis=1)


def first_feature(core, step):
    return (iota((16, LANES), 1) + (core * KDEV + step * KTILE)) * as_i32(K_STEP)


def sign_kernel(where_ref, seeds_ref, base_ref, sign_hbm, made_ref, sems):
    chip, core = where_ref[0], where_ref[1]
    row = iota((LANES, LANES), 0)
    for tile in range(TILES):
        column = chip * COLS + tile * LANES
        is_a = column < MODEL_WIDTH
        f = jnp.maximum(column - MODEL_WIDTH, 0)
        width = width_of(chip, tile)
        block = jnp.where(is_a, column // A_WIDTH, f // B_WIDTH)
        into = jnp.where(is_a, 0, f - f // B_WIDTH * B_WIDTH)
        after = jnp.minimum(block + 1, BLOCKS - 1)
        place = row + into
        over = place >= width
        seed = jnp.where(over, seeds_ref[after], seeds_ref[block])
        place = jnp.where(over, place - width, place)
        start = jnp.where(is_a, 0, RANK * A_WIDTH)
        base = (place + start) * as_i32(Q_STEP) + seed
        base_ref[tile * LANES : (tile + 1) * LANES] = base

    def send(i):
        slot = lax.rem(i, 2)
        return pltpu.make_async_copy(made_ref.at[slot], sign_hbm.at[i], sems.at[slot])

    def fill(i, carry):
        @pl.when(i >= 2)
        def _():
            send(i - 2).wait()

        slot = lax.rem(i, 2)
        tile, p = i // EARLY, lax.rem(i, EARLY)
        upper = None
        for row, signs in signs_of(base_ref, chip, p, first_feature(core, tile)):
            if row % 32:
                both = jnp.concatenate([upper, signs], axis=0)
                made_ref[slot, row - 16 : row + 16] = both.astype(F8)
            upper = signs
        send(i).start()
        return carry

    lax.fori_loop(0, NX * EARLY, fill, 0)
    send(NX * EARLY - 2).wait()
    send(NX * EARLY - 1).wait()


def arrange(ref, vec_ref):
    to, at = iota((256, 256), 0), iota((256, 256), 1)
    source = lax.rem(to, 16) // EXMAX * ROWS + lax.rem(to, EXMAX) * RANK + to // 16
    order = (at == source).astype(F32).astype(BF16)
    for y in range(NY):
        rows = ref[NX * y : NX * (y + 1)].reshape(NX * ROWS, COLS)
        rows = jnp.dot(order, rows, preferred_element_type=F32).astype(BF16)
        lo = y * CUT_SLOTS
        for r in range(RANK):
            vec_ref[r // 2, lo : lo + CUT_SLOTS, (r % 2) * COLS : (r % 2 + 1) * COLS] = rows[
                r * CUT_SLOTS : (r + 1) * CUT_SLOTS
            ]


def arrange_kernel(in_ref, out_ref):
    arrange(in_ref, out_ref)


def sketch_kernel(
    where_ref, base_ref, sign_hbm, mine_ref, partner_ref, out_ref, vec_ref, acc_ref, sign_ref, sems
):
    chip, core = where_ref[0], where_ref[1]

    def fetch(i):
        slot = lax.rem(i, 2 * EARLY)
        return pltpu.make_async_copy(sign_hbm.at[i], sign_ref.at[slot], sems.at[slot])

    for i in range(2):
        fetch(i).start()
    arrange(partner_ref, vec_ref)
    for i in range(2, EARLY):
        fetch(i).start()

    def vectors(p, q):
        return jnp.concatenate(
            [mine_ref[p, :, q : q + DEPTH], vec_ref[p, :, q : q + DEPTH]], axis=0
        )

    def tile(step, carry):
        feature = first_feature(core, step)
        acc_ref[...] = jnp.zeros_like(acc_ref)

        @pl.when(step + 1 < NX)
        def _():
            for i in range(EARLY):
                fetch((step + 1) * EARLY + i).start()

        chunks = range(0, 2 * COLS, DEPTH)
        stored = [(p, q) for p in range(EARLY) for q in chunks]
        fresh = [(p, q) for p in range(EARLY, PAIRS) for q in chunks]
        made = iter(())
        for j, (p, q) in enumerate(fresh):
            if q == 0:
                made = signs_of(base_ref, chip, p, feature)
            late = jnp.concatenate([next(made)[1] for _ in range(DEPTH // 16)], axis=0)
            sums = jnp.dot(vectors(p, q), late, preferred_element_type=F32)
            for e, at in stored[j * len(stored) // len(fresh) : (j + 1) * len(stored) // len(fresh)]:
                n = step * EARLY + e
                if at == 0:
                    fetch(n).wait()
                signs = sign_ref[lax.rem(n, 2 * EARLY), at : at + DEPTH].astype(BF16)
                sums = sums + jnp.dot(vectors(e, at), signs, preferred_element_type=F32)
            acc_ref[...] += sums
        total = acc_ref[...].astype(BF16)
        for half in range(NCORE):
            to_core = core if half == 0 else 1 - core
            for y in range(NY):
                lo = half * CHIPS * EXMAX + y * CUT_SLOTS
                out_ref[y, to_core, step] = total[lo : lo + CUT_SLOTS]
        return carry

    lax.fori_loop(0, NX, tile, 0)


def route_kernel(first_hbm, in_ref, out_ref, first_ref, sem):
    copy = pltpu.make_async_copy(first_hbm, first_ref, sem)
    copy.start()
    sums = []
    for c in range(NCORE):
        total = jnp.zeros((CUT_SLOTS, KTILE), F32)
        for y in range(NY):
            for x in range(NX):
                total = total + in_ref[(y * NCORE + c) * NX + x].astype(F32)
        sums.append(total.astype(BF16))
    stacked = jnp.concatenate(
        [
            sums[c][:, u * LANES : (u + 1) * LANES]
            for c in range(NCORE)
            for u in range(KTILE // LANES)
        ],
        axis=0,
    )
    z = lax.axis_index("z")
    copy.wait()
    width = PIECES * CUT_SLOTS
    row, col = iota((EXAMPLES * PIECES, width), 0), iota((EXAMPLES * PIECES, width), 1)
    slot = lax.rem(col, CUT_SLOTS)
    example = jnp.full(row.shape, -1, I32)
    for x in range(NX):
        cut = x * NZ + z
        number = first_ref[cut] + lax.rem(slot, EXMAX)
        number = jnp.where(number < first_ref[cut + 1], number, -1)
        example = jnp.where(slot // EXMAX == x, number, example)
    hit = (row // PIECES == example) & (lax.rem(row, PIECES) == col // CUT_SLOTS)
    routed = jnp.dot(hit.astype(F32).astype(BF16), stacked, preferred_element_type=F32)
    out_ref[...] = routed.astype(BF16).reshape(out_ref.shape)


def finish_kernel(in_ref, out_ref):
    scale = float(RANK * (MODEL_WIDTH + HIDDEN_UNITS) * TOK_DEV) ** (-0.5)
    per = KTILE // LANES
    for x in range(NX):
        total = jnp.zeros(in_ref.shape[1:], F32)
        for z in range(NZ):
            total = total + in_ref[x * NZ + z].astype(F32)
        total = total * scale
        for p in range(2):
            for c in range(NCORE):
                for u in range(per):
                    row = p * PIECES + c * per + u
                    lo = c * KDEV + x * KTILE + u * LANES
                    out_ref[p : p + 1, lo : lo + LANES] = total[row : row + 1]


VMEM = pl.BlockSpec(memory_space=pltpu.VMEM)
SMEM = pl.BlockSpec(memory_space=pltpu.SMEM)
HBM = pl.BlockSpec(memory_space=pltpu.HBM)


def in_hbm(array):
    return pltpu.with_memory_space_constraint(array, pltpu.HBM)


def params(mib):
    return pltpu.CompilerParams(vmem_limit_bytes=mib << 20)


def body(acts, gouts, adapter_down, adapter_up, token_example, cut_first, seeds):
    y, core, x = (lax.axis_index(name) for name in ("y", "core", "x"))
    grads = pl.pallas_call(
        gradient_kernel,
        out_shape=pltpu.HBM((CHIPS, ROWS, COLS), BF16),
        in_specs=[HBM] * 6,
        out_specs=HBM,
        scratch_shapes=[
            pltpu.VMEM((1, TOK_DEV), I32),
            pltpu.SMEM((cut_first.shape[0],), I32),
            pltpu.VMEM(acts.shape, BF16),
            pltpu.VMEM(gouts.shape, BF16),
            pltpu.VMEM((RANK, MODEL_WIDTH), BF16),
            pltpu.VMEM(adapter_up.shape, BF16),
            pltpu.VMEM((CHIPS, ROWS, COLS), BF16),
            pltpu.SemaphoreType.DMA((5 + len(GROUPS) - 1,)),
            pltpu.SemaphoreType.DMA((CHIPS,)),
        ],
        compiler_params=params(16),
        name="gradients",
    )(*(in_hbm(a) for a in (token_example.reshape(1, TOK_DEV), cut_first, acts, gouts, adapter_down.T, adapter_up)))
    where = jnp.stack([(y * NX + x).astype(I32), core.astype(I32)])
    where, seeds, grads = lax.optimization_barrier((where, seeds, grads))
    own = lax.all_to_all(grads, ("y", "x"), 0, 0, tiled=True)
    base, early = pl.pallas_call(
        sign_kernel,
        out_shape=(
            pltpu.VMEM((COLS, LANES), I32),
            pltpu.HBM((NX * EARLY, 2 * COLS, KTILE), F8),
        ),
        in_specs=[SMEM, SMEM],
        out_specs=(VMEM, HBM),
        scratch_shapes=[
            pltpu.VMEM((2, 2 * COLS, KTILE), F8),
            pltpu.SemaphoreType.DMA((2,)),
        ],
        cost_estimate=pl.CostEstimate(flops=20_000_000_000, bytes_accessed=0, transcendentals=0),
        compiler_params=params(16),
        name="signs",
    )(where, seeds)
    own, base = lax.optimization_barrier((own, base))
    partner = lax.ppermute(own, "core", [(0, 1), (1, 0)])
    mine = pl.pallas_call(
        arrange_kernel,
        out_shape=jax.ShapeDtypeStruct((PAIRS, SLOTS // NCORE, 2 * COLS), BF16),
        in_specs=[VMEM],
        out_specs=VMEM,
        cost_estimate=pl.CostEstimate(flops=1_500_000_000, bytes_accessed=0, transcendentals=0),
        compiler_params=params(16),
        name="arrange",
    )(own)
    parts = pl.pallas_call(
        sketch_kernel,
        out_shape=jax.ShapeDtypeStruct((NY, NCORE, NX, CUT_SLOTS, KTILE), BF16),
        in_specs=[SMEM, VMEM, HBM, VMEM, VMEM],
        out_specs=VMEM,
        scratch_shapes=[
            pltpu.VMEM((PAIRS, SLOTS // NCORE, 2 * COLS), BF16),
            pltpu.VMEM((SLOTS, KTILE), F32),
            pltpu.VMEM((2 * EARLY, 2 * COLS, KTILE), F8),
            pltpu.SemaphoreType.DMA((2 * EARLY,)),
        ],
        compiler_params=params(40),
        name="sketch",
    )(where, base, in_hbm(early), mine, partner)
    parts = parts.reshape(NY * NCORE * NX, CUT_SLOTS, KTILE)
    parts = lax.all_to_all(parts, ("y", "core", "x"), 0, 0, tiled=True)
    routed = pl.pallas_call(
        route_kernel,
        out_shape=jax.ShapeDtypeStruct((NX * NZ, 2 * PIECES, LANES), BF16),
        in_specs=[HBM, VMEM],
        out_specs=VMEM,
        scratch_shapes=[pltpu.SMEM((cut_first.shape[0],), I32), pltpu.SemaphoreType.DMA],
        compiler_params=params(32),
        name="route",
    )(in_hbm(cut_first), parts)
    routed = lax.all_to_all(routed, ("x", "z"), 0, 0, tiled=True)
    return pl.pallas_call(
        finish_kernel,
        out_shape=jax.ShapeDtypeStruct((2, SKETCH), F32),
        in_specs=[VMEM],
        out_specs=VMEM,
        compiler_params=params(32),
        name="finish",
    )(routed)


def solution(mesh):
    fine = Mesh(mesh.devices.reshape(NY, NCORE, NX, NZ), ("y", "core", "x", "z"))
    every = ("y", "core", "x", "z")
    in_specs = (P(every, None), P(every, None), P(), P(), P(every), P(("y", "core")), P())
    return jax.shard_map(body, mesh=fine, in_specs=in_specs, out_specs=P(every, None), check_vma=False)
```

```python
import jax
import jax.numpy as jnp
import numpy as np
from jax import lax
from jax.experimental import pallas as pl
from jax.experimental.pallas import tpu as pltpu
from jax.sharding import Mesh
from jax.sharding import PartitionSpec as P

MODEL_WIDTH = 4096
HIDDEN_UNITS = 14336
RANK = 16
SKETCH = 4096
BLOCKS = 32
TOK_DEV = 128
EXMAX = 4
EXAMPLES = 64
NY, NCORE, NX, NZ = 4, 2, 4, 8
CHIPS = NY * NX
COLS = (MODEL_WIDTH + HIDDEN_UNITS) // CHIPS
ROWS = EXMAX * RANK
LANES = 128
TILES = COLS // LANES
A_WIDTH = MODEL_WIDTH // BLOCKS
B_WIDTH = HIDDEN_UNITS // BLOCKS
PAIRS = RANK // 2
SLOTS = NCORE * CHIPS * EXMAX
KDEV = SKETCH // NCORE
KTILE = KDEV // NX
CUT_SLOTS = NX * EXMAX
PIECES = NCORE * KTILE // LANES
GROUPS = (3, 6, 9, 13, 16)
DEPTH = 256
EARLY = 7


def as_i32(value):
    value &= 0xFFFFFFFF
    return np.int32(value - (1 << 32) if value >= 1 << 31 else value)


Q_STEP = 1640531527
K_STEP = 668265263
MULT = as_i32(739982445 << 11)
NT = (((1,), (1,)), ((), ()))
F32 = jnp.float32
BF16 = jnp.bfloat16
I32 = jnp.int32
F8 = jnp.float8_e4m3fn


def iota(shape, dim):
    return lax.broadcasted_iota(I32, shape, dim)


def gradient_kernel(
    tok_hbm, first_hbm, act_hbm, gout_hbm, down_hbm, up_hbm, out_hbm,
    tok_ref, first_ref, act_ref, gout_ref, down_ref, up_ref, made_ref, sems, sent,
):
    copies = [
        pltpu.make_async_copy(src, dst, sems.at[i])
        for i, (src, dst) in enumerate(
            (
                (down_hbm, down_ref),
                (act_hbm, act_ref),
                (tok_hbm, tok_ref),
                (first_hbm, first_ref),
                (up_hbm, up_ref),
            )
        )
    ]
    for lo, hi in zip(GROUPS[:-1], GROUPS[1:]):
        columns = slice(max(lo * COLS - MODEL_WIDTH, 0), hi * COLS - MODEL_WIDTH)
        copies.append(
            pltpu.make_async_copy(
                gout_hbm.at[:, columns], gout_ref.at[:, columns], sems.at[len(copies)]
            )
        )
    for copy in copies:
        copy.start()
    expand = (lax.rem(iota((ROWS, RANK), 0), RANK) == iota((ROWS, RANK), 1)).astype(F32).astype(BF16)
    for copy in copies[:4]:
        copy.wait()
    cut = lax.axis_index("x") * NZ + lax.axis_index("z")
    slot = tok_ref[...] - first_ref[cut]
    mine = (iota((ROWS, TOK_DEV), 0) // RANK) == slot

    def spread(factor):
        rows = lax.dot_general(expand, factor.astype(BF16), NT, preferred_element_type=F32)
        return jnp.where(mine, rows, 0.0).astype(BF16)

    spread_down = spread(
        lax.dot_general(act_ref[...], down_ref[...], NT, preferred_element_type=F32)
    )
    copies[4].wait()
    def send(chip):
        return pltpu.make_async_copy(made_ref.at[chip], out_hbm.at[chip], sent.at[chip])

    up = jnp.zeros((TOK_DEV, RANK), F32)
    for group, (first, last) in enumerate(zip(GROUPS[:-1], GROUPS[1:])):
        copies[5 + group].wait()
        for chip in range(first, last):
            lo, hi = max(chip * COLS - MODEL_WIDTH, 0), (chip + 1) * COLS - MODEL_WIDTH
            up = up + lax.dot_general(
                gout_ref[:, lo:hi], up_ref[:, lo:hi], NT, preferred_element_type=F32
            )
            part = jnp.dot(spread_down, gout_ref[:, lo:hi], preferred_element_type=F32)
            made_ref[chip, :, COLS - (hi - lo) :] = part.astype(BF16)
            if chip > GROUPS[0]:
                send(chip).start()
    spread_up = spread(up)
    for chip in range(GROUPS[0] + 1):
        lo, hi = chip * COLS, min((chip + 1) * COLS, MODEL_WIDTH)
        part = jnp.dot(spread_up, act_ref[:, lo:hi], preferred_element_type=F32)
        made_ref[chip, :, : hi - lo] = part.astype(BF16)
        send(chip).start()
    for chip in range(CHIPS):
        send(chip).wait()


def width_of(chip, tile):
    return jnp.where(chip * COLS + tile * LANES < MODEL_WIDTH, A_WIDTH, B_WIDTH)


def signs_of(base_ref, chip, p, feature):
    for half in range(2):
        for tile in range(TILES):
            shift = width_of(chip, tile) * (2 * p + half) * as_i32(Q_STEP)
            there = [
                feature + (as_i32(k * K_STEP) + shift) for k in range(0, KTILE, LANES)
            ]
            for row in range(tile * LANES, (tile + 1) * LANES, 16):
                base = base_ref[row : row + 16]
                signs = []
                for here in there:
                    h = base + here
                    h = (h ^ lax.shift_right_logical(h, np.int32(15))) * MULT
                    signs.append(jnp.where(h < 0, BF16(1), BF16(-1)))
                yield half * COLS + row, jnp.concatenate(signs, axis=1)


def first_feature(core, step):
    return (iota((16, LANES), 1) + (core * KDEV + step * KTILE)) * as_i32(K_STEP)


def sign_kernel(where_ref, seeds_ref, base_ref, sign_hbm, made_ref, sems):
    chip, core = where_ref[0], where_ref[1]
    row = iota((LANES, LANES), 0)
    for tile in range(TILES):
        column = chip * COLS + tile * LANES
        is_a = column < MODEL_WIDTH
        f = jnp.maximum(column - MODEL_WIDTH, 0)
        width = width_of(chip, tile)
        block = jnp.where(is_a, column // A_WIDTH, f // B_WIDTH)
        into = jnp.where(is_a, 0, f - f // B_WIDTH * B_WIDTH)
        after = jnp.minimum(block + 1, BLOCKS - 1)
        place = row + into
        over = place >= width
        seed = jnp.where(over, seeds_ref[after], seeds_ref[block])
        place = jnp.where(over, place - width, place)
        start = jnp.where(is_a, 0, RANK * A_WIDTH)
        base = (place + start) * as_i32(Q_STEP) + seed
        base_ref[tile * LANES : (tile + 1) * LANES] = base

    def send(i):
        slot = lax.rem(i, 2)
        return pltpu.make_async_copy(made_ref.at[slot], sign_hbm.at[i], sems.at[slot])

    def fill(i, carry):
        @pl.when(i >= 2)
        def _():
            send(i - 2).wait()

        slot = lax.rem(i, 2)
        tile, p = i // EARLY, lax.rem(i, EARLY)
        upper = None
        for row, signs in signs_of(base_ref, chip, p, first_feature(core, tile)):
            if row % 32:
                both = jnp.concatenate([upper, signs], axis=0)
                made_ref[slot, row - 16 : row + 16] = both.astype(F8)
            upper = signs
        send(i).start()
        return carry

    lax.fori_loop(0, NX * EARLY, fill, 0)
    send(NX * EARLY - 2).wait()
    send(NX * EARLY - 1).wait()


def arrange(ref, vec_ref):
    to, at = iota((256, 256), 0), iota((256, 256), 1)
    source = lax.rem(to, 16) // EXMAX * ROWS + lax.rem(to, EXMAX) * RANK + to // 16
    order = (at == source).astype(F32).astype(BF16)
    for y in range(NY):
        rows = ref[NX * y : NX * (y + 1)].reshape(NX * ROWS, COLS)
        rows = jnp.dot(order, rows, preferred_element_type=F32).astype(BF16)
        lo = y * CUT_SLOTS
        for r in range(RANK):
            vec_ref[r // 2, lo : lo + CUT_SLOTS, (r % 2) * COLS : (r % 2 + 1) * COLS] = rows[
                r * CUT_SLOTS : (r + 1) * CUT_SLOTS
            ]


def arrange_kernel(in_ref, out_ref):
    arrange(in_ref, out_ref)


def sketch_kernel(
    where_ref, base_ref, sign_hbm, mine_ref, partner_ref, out_ref, vec_ref, acc_ref, sign_ref, sems
):
    chip, core = where_ref[0], where_ref[1]

    def fetch(i):
        slot = lax.rem(i, 2 * EARLY)
        return pltpu.make_async_copy(sign_hbm.at[i], sign_ref.at[slot], sems.at[slot])

    for i in range(2):
        fetch(i).start()
    arrange(partner_ref, vec_ref)
    for i in range(2, EARLY):
        fetch(i).start()

    def vectors(p, q):
        return jnp.concatenate(
            [mine_ref[p, :, q : q + DEPTH], vec_ref[p, :, q : q + DEPTH]], axis=0
        )

    def tile(step, carry):
        feature = first_feature(core, step)
        acc_ref[...] = jnp.zeros_like(acc_ref)

        @pl.when(step + 1 < NX)
        def _():
            for i in range(EARLY):
                fetch((step + 1) * EARLY + i).start()

        chunks = range(0, 2 * COLS, DEPTH)
        stored = [(p, q) for p in range(EARLY) for q in chunks]
        fresh = [(p, q) for p in range(EARLY, PAIRS) for q in chunks]
        made = iter(())
        for j, (p, q) in enumerate(fresh):
            if q == 0:
                made = signs_of(base_ref, chip, p, feature)
            late = jnp.concatenate([next(made)[1] for _ in range(DEPTH // 16)], axis=0)
            sums = jnp.dot(vectors(p, q), late, preferred_element_type=F32)
            for e, at in stored[j * len(stored) // len(fresh) : (j + 1) * len(stored) // len(fresh)]:
                n = step * EARLY + e
                if at == 0:
                    fetch(n).wait()
                signs = sign_ref[lax.rem(n, 2 * EARLY), at : at + DEPTH]
                sums = sums + jnp.dot(vectors(e, at), signs, preferred_element_type=F32)
            acc_ref[...] += sums
        total = acc_ref[...].astype(BF16)
        for half in range(NCORE):
            to_core = core if half == 0 else 1 - core
            for y in range(NY):
                lo = half * CHIPS * EXMAX + y * CUT_SLOTS
                out_ref[y, to_core, step] = total[lo : lo + CUT_SLOTS]
        return carry

    lax.fori_loop(0, NX, tile, 0)


def route_kernel(first_hbm, in_ref, out_ref, first_ref, sem):
    copy = pltpu.make_async_copy(first_hbm, first_ref, sem)
    copy.start()
    sums = []
    for c in range(NCORE):
        total = jnp.zeros((CUT_SLOTS, KTILE), F32)
        for y in range(NY):
            for x in range(NX):
                total = total + in_ref[(y * NCORE + c) * NX + x].astype(F32)
        sums.append(total.astype(BF16))
    stacked = jnp.concatenate(
        [
            sums[c][:, u * LANES : (u + 1) * LANES]
            for c in range(NCORE)
            for u in range(KTILE // LANES)
        ],
        axis=0,
    )
    z = lax.axis_index("z")
    copy.wait()
    width = PIECES * CUT_SLOTS
    row, col = iota((EXAMPLES * PIECES, width), 0), iota((EXAMPLES * PIECES, width), 1)
    slot = lax.rem(col, CUT_SLOTS)
    example = jnp.full(row.shape, -1, I32)
    for x in range(NX):
        cut = x * NZ + z
        number = first_ref[cut] + lax.rem(slot, EXMAX)
        number = jnp.where(number < first_ref[cut + 1], number, -1)
        example = jnp.where(slot // EXMAX == x, number, example)
    hit = (row // PIECES == example) & (lax.rem(row, PIECES) == col // CUT_SLOTS)
    routed = jnp.dot(hit.astype(F32).astype(BF16), stacked, preferred_element_type=F32)
    out_ref[...] = routed.astype(BF16).reshape(out_ref.shape)


def finish_kernel(in_ref, out_ref):
    scale = float(RANK * (MODEL_WIDTH + HIDDEN_UNITS) * TOK_DEV) ** (-0.5)
    per = KTILE // LANES
    for x in range(NX):
        total = jnp.zeros(in_ref.shape[1:], F32)
        for z in range(NZ):
            total = total + in_ref[x * NZ + z].astype(F32)
        total = total * scale
        for p in range(2):
            for c in range(NCORE):
                for u in range(per):
                    row = p * PIECES + c * per + u
                    lo = c * KDEV + x * KTILE + u * LANES
                    out_ref[p : p + 1, lo : lo + LANES] = total[row : row + 1]


VMEM = pl.BlockSpec(memory_space=pltpu.VMEM)
SMEM = pl.BlockSpec(memory_space=pltpu.SMEM)
HBM = pl.BlockSpec(memory_space=pltpu.HBM)


def in_hbm(array):
    return pltpu.with_memory_space_constraint(array, pltpu.HBM)


def params(mib):
    return pltpu.CompilerParams(vmem_limit_bytes=mib << 20)


def body(acts, gouts, adapter_down, adapter_up, token_example, cut_first, seeds):
    y, core, x = (lax.axis_index(name) for name in ("y", "core", "x"))
    grads = pl.pallas_call(
        gradient_kernel,
        out_shape=pltpu.HBM((CHIPS, ROWS, COLS), BF16),
        in_specs=[HBM] * 6,
        out_specs=HBM,
        scratch_shapes=[
            pltpu.VMEM((1, TOK_DEV), I32),
            pltpu.SMEM((cut_first.shape[0],), I32),
            pltpu.VMEM(acts.shape, BF16),
            pltpu.VMEM(gouts.shape, BF16),
            pltpu.VMEM((RANK, MODEL_WIDTH), BF16),
            pltpu.VMEM(adapter_up.shape, BF16),
            pltpu.VMEM((CHIPS, ROWS, COLS), BF16),
            pltpu.SemaphoreType.DMA((5 + len(GROUPS) - 1,)),
            pltpu.SemaphoreType.DMA((CHIPS,)),
        ],
        compiler_params=params(16),
        name="gradients",
    )(*(in_hbm(a) for a in (token_example.reshape(1, TOK_DEV), cut_first, acts, gouts, adapter_down.T, adapter_up)))
    where = jnp.stack([(y * NX + x).astype(I32), core.astype(I32)])
    where, seeds, grads = lax.optimization_barrier((where, seeds, grads))
    own = lax.all_to_all(grads, ("y", "x"), 0, 0, tiled=True)
    base, early = pl.pallas_call(
        sign_kernel,
        out_shape=(
            pltpu.VMEM((COLS, LANES), I32),
            pltpu.HBM((NX * EARLY, 2 * COLS, KTILE), F8),
        ),
        in_specs=[SMEM, SMEM],
        out_specs=(VMEM, HBM),
        scratch_shapes=[
            pltpu.VMEM((2, 2 * COLS, KTILE), F8),
            pltpu.SemaphoreType.DMA((2,)),
        ],
        cost_estimate=pl.CostEstimate(flops=20_000_000_000, bytes_accessed=0, transcendentals=0),
        compiler_params=params(16),
        name="signs",
    )(where, seeds)
    own, base = lax.optimization_barrier((own, base))
    partner = lax.ppermute(own, "core", [(0, 1), (1, 0)])
    mine = pl.pallas_call(
        arrange_kernel,
        out_shape=jax.ShapeDtypeStruct((PAIRS, SLOTS // NCORE, 2 * COLS), BF16),
        in_specs=[VMEM],
        out_specs=VMEM,
        cost_estimate=pl.CostEstimate(flops=1_500_000_000, bytes_accessed=0, transcendentals=0),
        compiler_params=params(16),
        name="arrange",
    )(own)
    parts = pl.pallas_call(
        sketch_kernel,
        out_shape=jax.ShapeDtypeStruct((NY, NCORE, NX, CUT_SLOTS, KTILE), BF16),
        in_specs=[SMEM, VMEM, HBM, VMEM, VMEM],
        out_specs=VMEM,
        scratch_shapes=[
            pltpu.VMEM((PAIRS, SLOTS // NCORE, 2 * COLS), BF16),
            pltpu.VMEM((SLOTS, KTILE), F32),
            pltpu.VMEM((2 * EARLY, 2 * COLS, KTILE), F8),
            pltpu.SemaphoreType.DMA((2 * EARLY,)),
        ],
        compiler_params=params(40),
        name="sketch",
    )(where, base, in_hbm(early), mine, partner)
    parts = parts.reshape(NY * NCORE * NX, CUT_SLOTS, KTILE)
    parts = lax.all_to_all(parts, ("y", "core", "x"), 0, 0, tiled=True)
    routed = pl.pallas_call(
        route_kernel,
        out_shape=jax.ShapeDtypeStruct((NX * NZ, 2 * PIECES, LANES), BF16),
        in_specs=[HBM, VMEM],
        out_specs=VMEM,
        scratch_shapes=[pltpu.SMEM((cut_first.shape[0],), I32), pltpu.SemaphoreType.DMA],
        compiler_params=params(32),
        name="route",
    )(in_hbm(cut_first), parts)
    routed = lax.all_to_all(routed, ("x", "z"), 0, 0, tiled=True)
    return pl.pallas_call(
        finish_kernel,
        out_shape=jax.ShapeDtypeStruct((2, SKETCH), F32),
        in_specs=[VMEM],
        out_specs=VMEM,
        compiler_params=params(32),
        name="finish",
    )(routed)


def solution(mesh):
    fine = Mesh(mesh.devices.reshape(NY, NCORE, NX, NZ), ("y", "core", "x", "z"))
    every = ("y", "core", "x", "z")
    in_specs = (P(every, None), P(every, None), P(), P(), P(every), P(("y", "core")), P())
    return jax.shard_map(body, mesh=fine, in_specs=in_specs, out_specs=P(every, None), check_vma=False)
```
